32 devices in a mesh: seq: 16 (over z, y, core), hid: 2 (over x).
Axes of the slice: x: 2, y: 2, z: 4, core: 2. Of those that a mesh axis runs over, the one named last changes fastest.
Arguments:
- queries: bfloat16 [6144, 3072], P('seq', 'hid'), may hold values from -6 to 6
- keys: bfloat16 [6144, 3072], P('seq', 'hid'), may hold values from -4 to 4
- values: bfloat16 [6144, 3072], P('seq', 'hid'), may hold values from -6 to 6
- residual: bfloat16 [6144, 3072], P('seq', 'hid'), may hold values from -24 to 24
- w_in: bfloat16 [3072, 6144], P(None, 'hid'), may hold values from -0.109375 to 0.109375
- w_out: bfloat16 [6144, 3072], P('hid', 'seq'), may hold values from -0.078125 to 0.078125
- mod_scale: float32 [3072], replicated, may hold values from -0.5 to 0.5
- mod_gate: float32 [3072], replicated, may hold values from 0.5 to 1.5
- slot_tiles: int32 [16], replicated, may hold values from 0 to 15, as said below
- key_tiles: int32 [16, 27], replicated, may hold values from -1 to 15, as said below
Outputs:
- block_out: bfloat16 [6144, 3072], P('seq', 'hid')
The draws below stay inside these ranges and needn't reach their ends.
Inputs may be any that keep to these rules, and one draw needn't show every extreme that they name: slot_tiles is a permutation of the tiles of a grid of 8 x 1 x 2, tile id (t + h) * 2 + w; two tiles that differ by at most one along every grid dimension sit at most 3 slots apart. `key_tiles`: row q lists distinct tile ids, each within one step of tile q along every grid dimension, in a fixed order of the 27 offsets; column 13 is q itself; other entries are -1.
All inputs are finite; a program needn't handle non-finite values.
Results may differ from the reference program's by a relative error of at most 0.0052.
Values may be sent and summed in bfloat16 or wider, within the bound.
A program may use at most 128 MiB of HBM per device.

```python
import jax
import jax.numpy as jnp
from jax import lax

D = 3072
HEADS = 24
HEAD_DIM = 128
FF = 6144
GRID_H = 1
GRID_W = 2
WINDOW = 27
TOK_DEV = 384
TILE = 384
REACH = 3
TOKENS = 6144
TILES = 16
FRAMES = 8
N_SEQ = 16


def draw_queries(key, part):
    key = jax.random.fold_in(key, 11)
    drawn = jnp.clip(jax.random.normal(key, (TOKENS, D), jnp.float32), -4.0, 4.0)
    return drawn.astype(jnp.bfloat16)


def draw_keys(key, part):
    key = jax.random.fold_in(key, 13)
    drawn = jnp.clip(jax.random.normal(key, (TOKENS, D), jnp.float32), -4.0, 4.0)
    return drawn.astype(jnp.bfloat16)


def draw_residual(key, part):
    key = jax.random.fold_in(key, 17)
    row_key = jax.random.fold_in(key, 1)
    col_key = jax.random.fold_in(key, 2)
    row_scale = jnp.exp(jax.random.uniform(row_key, (TOKENS, 1), jnp.float32, -1.2, 1.2))
    col_scale = jnp.exp(jax.random.uniform(col_key, (1, D), jnp.float32, -0.7, 0.7))
    base = jnp.clip(jax.random.normal(key, (TOKENS, D), jnp.float32), -3.0, 3.0)
    return (base * row_scale * col_scale).astype(jnp.bfloat16)


def draw_slot_tiles(key, part):
    key = jax.random.fold_in(key, 5)
    flips = jax.random.randint(key, (3,), 0, 2)
    slot_index = jnp.arange(TILES, dtype=jnp.int32)
    frame = slot_index // (GRID_H * GRID_W)
    row_pos = slot_index // GRID_W % GRID_H
    col_pos = slot_index % GRID_W
    frame = jnp.where(flips[0] == 1, FRAMES - 1 - frame, frame)
    row_pos = jnp.where(flips[1] == 1, GRID_H - 1 - row_pos, row_pos)
    col_pos = jnp.where(flips[2] == 1, GRID_W - 1 - col_pos, col_pos)
    return ((frame * GRID_H + row_pos) * GRID_W + col_pos).astype(jnp.int32)


def draw_key_tiles(key, part):
    key = jax.random.fold_in(key, 7)
    keep = jax.random.randint(key, (TILES, WINDOW), 0, 4) > 0
    tile_id = jnp.arange(TILES, dtype=jnp.int32)[:, None]
    offset = jnp.arange(WINDOW, dtype=jnp.int32)[None, :]
    frame = tile_id // (GRID_H * GRID_W) + offset // 9 - 1
    row_pos = tile_id // GRID_W % GRID_H + offset // 3 % 3 - 1
    col_pos = tile_id % GRID_W + offset % 3 - 1
    inside = (frame >= 0) & (frame < FRAMES) & (row_pos >= 0) & (row_pos < GRID_H) & (col_pos >= 0) & (col_pos < GRID_W)
    usable = inside & (keep | (offset == 13))
    return jnp.where(usable, (frame * GRID_H + row_pos) * GRID_W + col_pos, -1).astype(jnp.int32)


def block_levels(stream_key, shape, cuts, low, top_value):
    level = 1.0
    for axis_at, blocks in cuts:
        draws = jax.random.uniform(jax.random.fold_in(jax.random.fold_in(stream_key, 6), axis_at), (blocks,), jnp.float32, low / len(cuts), top_value / len(cuts))
        level = level * jnp.repeat(jnp.exp(draws), shape[axis_at] // blocks).reshape((-1,) + (1,) * (len(shape) - 1 - axis_at))
    return level


def noise(key, extent, scale, reach, shards=(), held_as=jnp.bfloat16):
    values = scale * jax.random.normal(key, extent, jnp.float32)
    if shards:
        values = values * block_levels(key, extent, shards, -0.22, 0.18)
    return jnp.clip(values, -reach, reach).astype(held_as)


def setup_inputs(seed: int = 0) -> dict:
    arg_keys = jax.random.split(jax.random.key(seed), 11)
    return {
        "queries": draw_queries(jax.random.fold_in(arg_keys[10], 71), 0),
        "keys": draw_keys(jax.random.fold_in(arg_keys[10], 71), 0),
        "values": noise(arg_keys[2], (TOKENS, D), 1.0, 6.0, ((0, 16), (1, 2))),
        "residual": draw_residual(jax.random.fold_in(arg_keys[10], 71), 0),
        "w_in": noise(arg_keys[4], (D, FF), D ** -0.5, 0.109375, ((1, 2),)),
        "w_out": noise(arg_keys[5], (FF, D), FF ** -0.5, 0.078125, ((0, 2), (1, 16))),
        "mod_scale": jnp.clip(jax.random.uniform(arg_keys[6], (D,), jnp.float32, -0.5, 0.5), -0.5, 0.5),
        "mod_gate": jnp.clip(jax.random.uniform(arg_keys[7], (D,), jnp.float32, 0.5, 1.5), 0.5, 1.5),
        "slot_tiles": draw_slot_tiles(jax.random.fold_in(arg_keys[10], 71), 0),
        "key_tiles": draw_key_tiles(jax.random.fold_in(arg_keys[10], 71), 0),
    }


def reference(queries, keys, values, residual, w_in, w_out, mod_scale, mod_gate, slot_tiles, key_tiles):
    tile_total = slot_tiles.shape[0]
    span = 2 * REACH + 1
    q_tiles = queries.reshape(tile_total, TILE, HEADS, HEAD_DIM)
    k_tiles = keys.reshape(tile_total, TILE, HEADS, HEAD_DIM)
    v_tiles = values.reshape(tile_total, TILE, HEADS, HEAD_DIM)

    def attend_tile(slot_index):
        near = slot_index - REACH + jnp.arange(span, dtype=jnp.int32)
        inside = (near >= 0) & (near < tile_total)
        near_safe = jnp.clip(near, 0, tile_total - 1).astype(jnp.int32)
        near_tiles = slot_tiles[near_safe]
        wanted = key_tiles[slot_tiles[slot_index]]
        listed = jnp.any(wanted[:, None] == near_tiles[None, :], axis=0) & inside
        k_rows = k_tiles[near_safe].reshape(span * TILE, HEADS, HEAD_DIM).astype(jnp.float32)
        v_rows = v_tiles[near_safe].reshape(span * TILE, HEADS, HEAD_DIM).astype(jnp.float32)
        row_ok = jnp.repeat(listed, TILE)
        q_rows = q_tiles[slot_index].astype(jnp.float32)
        scores = jnp.einsum('qhd,khd->hqk', q_rows, k_rows) * (1.0 / HEAD_DIM ** 0.5)
        scores = jnp.where(row_ok[None, None, :], scores, -jnp.inf)
        row_max = lax.optimization_barrier(jnp.max(scores, axis=-1, keepdims=True))
        probs = jnp.exp(scores - row_max)
        row_total = lax.optimization_barrier(jnp.sum(probs, axis=-1))
        probs_low = probs.astype(jnp.bfloat16)
        blended = jnp.einsum('hqk,khd->qhd', probs_low.astype(jnp.float32), v_rows)
        blended = blended / jnp.transpose(row_total)[:, :, None]
        return blended.reshape(TILE, D).astype(jnp.bfloat16)
    attn = lax.map(attend_tile, jnp.arange(tile_total, dtype=jnp.int32)).reshape(TOKENS, D)
    combined = (residual.astype(jnp.float32) + attn.astype(jnp.float32)).astype(jnp.bfloat16)

    def mlp_block(rows):
        wide = rows.astype(jnp.float32)
        square = lax.optimization_barrier(jnp.mean(wide * wide, axis=-1, keepdims=True))
        normed = (wide * lax.rsqrt(square + 1e-06) * (1.0 + mod_scale)).astype(jnp.bfloat16)
        inner = jnp.dot(normed, w_in, preferred_element_type=jnp.float32)
        hidden = jax.nn.gelu(inner, approximate=True).astype(jnp.bfloat16)
        return jnp.dot(hidden, w_out, preferred_element_type=jnp.float32)
    mlp = lax.map(mlp_block, combined.reshape(N_SEQ, TOK_DEV, D)).reshape(TOKENS, D)
    return (combined.astype(jnp.float32) + mod_gate * mlp).astype(jnp.bfloat16)
```

```python
import functools
import math

import jax
import jax.numpy as jnp
from jax import lax
from jax.experimental import pallas as pl
from jax.experimental.pallas import tpu as pltpu
from jax.sharding import PartitionSpec as P

HEAD_DIM = 128
TILE = 384
SLOTS = 6
GROUP = 256
W_CHUNK = 512
UNIT = 384
MESH = pl.DeviceIdType.MESH


def block_kernel(
    chips,
    q_ref, res_ref, bias_ref, scale_ref, gate_ref, k_hbm, v_hbm, win_hbm, wout_hbm,
    out_ref,
    kv, wout, win, comb, normed, hidden, term_out, term_in,
    local_sem, win_sem, near_s, near_r, far_s, far_r, own_s, own_r, cn_s, cn_r, cf_s, cf_r,
    x_s, x_r, ring_s, ring_r, cring_s, cring_r, wown_s, wown_r, term_s, term_r,
):
    seq = lax.axis_index("seq")
    hid = lax.axis_index("hid")
    chip, core = seq // 2, seq % 2
    odd = chip % 2
    rows, width = q_ref.shape
    depth = win_hbm.shape[0]
    units = win_hbm.shape[1]
    groups = width // GROUP
    w_rows = wout_hbm.shape[0]
    half_ring = chips // 2

    def at(chip_index, core_index):
        return {"seq": chip_index * 2 + core_index}

    mate = at(chip, 1 - core)
    near = at(chip + 1 - 2 * odd, core)
    step = 2 - 4 * odd
    has_far = (chip - step >= 0) & (chip - step < chips)
    has_fwd = (chip + step >= 0) & (chip + step < chips)
    ahead = at(chip + step, core)
    behind = at(chip - step, core)
    peer = {"hid": 1 - hid}

    place = jnp.where(odd == 0, chip // 2, chips - 1 - chip // 2)

    def ring_chip(position):
        position = (position + 2 * chips) % chips
        return jnp.where(position < half_ring, 2 * position, 2 * (chips - 1 - position) + 1)

    ring_next = at(ring_chip(place + 1), core)
    ring_prev = at(ring_chip(place - 1), core)

    near_row = (4 - 4 * odd) * TILE
    far_row = 4 * odd * TILE
    mid_row = 2 * TILE

    def kv_rows(base, which):
        return pl.ds(pl.multiple_of(base + which * TILE, TILE), TILE)

    def cols(g):
        return pl.ds(pl.multiple_of(g * GROUP, GROUP), GROUP)

    def remote(src, dst, send, recv, device):
        return pltpu.make_async_remote_copy(
            src_ref=src, dst_ref=dst, send_sem=send, recv_sem=recv,
            device_id=device, device_id_type=MESH,
        )

    def mine(g):
        return kv.at[:, kv_rows(mid_row, core), cols(g)]

    def near_copy(g):
        return remote(
            mine(g), kv.at[:, kv_rows(far_row, core), cols(g)], near_s.at[g], near_r.at[g], near
        )

    def far_copy(g):
        return remote(
            kv.at[:, kv_rows(near_row, core), cols(g)],
            kv.at[:, kv_rows(far_row, core), cols(g)], far_s.at[g], far_r.at[g], ahead,
        )

    def mate_copy(base, send, recv, g):
        part = kv.at[:, kv_rows(base, core), cols(g)]
        return remote(part, part, send.at[g], recv.at[g], mate)

    def own_copy(g):
        return mate_copy(mid_row, own_s, own_r, g)

    def cn_copy(g):
        return mate_copy(near_row, cn_s, cn_r, g)

    def cf_copy(g):
        return mate_copy(far_row, cf_s, cf_r, g)

    def comb_cols(g):
        return pl.ds(pl.multiple_of(hid * width + g * GROUP, GROUP), GROUP)

    def x_copy(g):
        part = comb.at[:, comb_cols(g)]
        return remote(part, part, x_s.at[g], x_r.at[g], peer)

    def wout_part(chip_index, core_index, lanes):
        row = pl.multiple_of((chip_index * 2 + core_index) * w_rows, w_rows)
        return wout.at[pl.ds(row, w_rows), lanes]

    def lanes_of(way, t):
        if t < half_ring:
            return pl.ds(0, units)
        return pl.ds(way * (units // 2), units // 2)

    def ring_copy(way, t):
        source = ring_chip(place - (t - 1) if way == 0 else place + (t - 1))
        part = wout_part(source, core, lanes_of(way, t))
        return remote(
            part, part, ring_s.at[way, t - 1], ring_r.at[way, t - 1],
            ring_next if way == 0 else ring_prev,
        )

    def ring_mate(way, t):
        source = ring_chip(place - t if way == 0 else place + t)
        part = wout_part(source, core, lanes_of(way, t))
        return remote(part, part, cring_s.at[way, t - 1], cring_r.at[way, t - 1], mate)

    def ring_step(t):
        for way in range(2):
            ring_copy(way, t).wait_recv()
            if t < half_ring:
                ring_copy(way, t + 1).start()
            ring_mate(way, t).start()

    def wown_copy():
        part = wout_part(chip, core, pl.ds(0, units))
        return remote(part, part, wown_s.at[0], wown_r.at[0], mate)

    def win_copy(j, slot):
        return pltpu.make_async_copy(
            win_hbm.at[:, pl.ds(pl.multiple_of(j * W_CHUNK, W_CHUNK), W_CHUNK)],
            win.at[slot], win_sem.at[slot],
        )

    def term_copy(j):
        return remote(term_out.at[j], term_in.at[j], term_s.at[j], term_r.at[j], peer)

    loads = [
        pltpu.make_async_copy(k_hbm, kv.at[0, kv_rows(mid_row, core), :], local_sem.at[0]),
        pltpu.make_async_copy(v_hbm, kv.at[1, kv_rows(mid_row, core), :], local_sem.at[1]),
        pltpu.make_async_copy(
            wout_hbm, wout_part(chip, core, pl.ds(0, units)), local_sem.at[2]
        ),
    ]
    for load in loads:
        load.start()
    win_copy(0, 0).start()
    win_copy(1, 1).start()

    barrier = pltpu.get_barrier_semaphore()
    for device in (mate, near, peer, ring_next, ring_prev):
        pl.semaphore_signal(barrier, inc=1, device_id=device, device_id_type=MESH)

    @pl.when(has_fwd)
    def _():
        pl.semaphore_signal(barrier, inc=1, device_id=ahead, device_id_type=MESH)

    @pl.when(has_far)
    def _():
        pl.semaphore_signal(barrier, inc=1, device_id=behind, device_id_type=MESH)

    pl.semaphore_wait(barrier, 5 + has_fwd.astype(jnp.int32) + has_far.astype(jnp.int32))

    loads[0].wait()
    loads[1].wait()

    def send_own(g, _):
        near_copy(g).start()
        own_copy(g).start()
        return 0

    lax.fori_loop(0, groups, send_own, 0)
    loads[2].wait()
    ring_copy(0, 1).start()
    ring_copy(1, 1).start()
    wown_copy().start()

    @pl.when(jnp.logical_not(has_far))
    def _():
        kv[:, pl.ds(pl.multiple_of(far_row, TILE), 2 * TILE), :] = jnp.zeros(
            (2, 2 * TILE, width), kv.dtype
        )

    def attend(g):
        def head(h, _):
            lanes = pl.ds(pl.multiple_of(g * GROUP + h * HEAD_DIM, HEAD_DIM), HEAD_DIM)
            scores = lax.dot_general(
                q_ref[:, lanes], kv[0, :, lanes], (((1,), (1,)), ((), ())),
                preferred_element_type=jnp.float32,
            )
            scores = scores * (1.0 / math.sqrt(HEAD_DIM)) + bias_ref[...]
            probs = jnp.exp(scores - jnp.max(scores, axis=-1, keepdims=True))
            total = jnp.sum(probs, axis=-1, keepdims=True)
            mixed = jnp.dot(
                probs.astype(jnp.bfloat16), kv[1, :, lanes], preferred_element_type=jnp.float32
            )
            attn = (mixed / total).astype(jnp.bfloat16)
            summed = res_ref[:, lanes].astype(jnp.float32) + attn.astype(jnp.float32)
            lanes_to = pl.ds(
                pl.multiple_of(hid * width + g * GROUP + h * HEAD_DIM, HEAD_DIM), HEAD_DIM
            )
            comb[:, lanes_to] = summed.astype(jnp.bfloat16)
            return 0

        lax.fori_loop(0, GROUP // HEAD_DIM, head, 0)

    def group_step(g, _):
        @pl.when(g < groups)
        def _():
            near_in = remote(
                mine(g), kv.at[:, kv_rows(near_row, core), cols(g)], near_s.at[g], near_r.at[g],
                near,
            )
            near_in.wait_recv()

            @pl.when(has_fwd)
            def _():
                far_copy(g).start()

            cn_copy(g).start()

        @pl.when(g >= 1)
        def _():
            prior = g - 1

            @pl.when(has_far)
            def _():
                far_copy(prior).wait_recv()
                cf_copy(prior).start()

            mate_in(own_r, mid_row, prior).wait_recv()
            mate_in(cn_r, near_row, prior).wait_recv()

            @pl.when(has_far)
            def _():
                mate_in(cf_r, far_row, prior).wait_recv()

            attend(prior)
            x_copy(prior).start()

        @pl.when(g == 3)
        def _():
            ring_step(1)

        return 0

    def mate_in(recv, base, g):
        part = kv.at[:, kv_rows(base, 1 - core), cols(g)]
        return remote(part, part, own_s.at[g], recv.at[g], mate)

    lax.fori_loop(0, groups + 1, group_step, 0)

    ring_step(2)

    def x_in(g, _):
        part = comb.at[:, pl.ds(pl.multiple_of((1 - hid) * width + g * GROUP, GROUP), GROUP)]
        remote(part, part, x_s.at[g], x_r.at[g], peer).wait_recv()
        return 0

    lax.fori_loop(0, groups, x_in, 0)

    norm_rows = 64

    def norm(i, _):
        block = pl.ds(pl.multiple_of(i * norm_rows, norm_rows), norm_rows)
        wide = comb[block, :].astype(jnp.float32)
        square = jnp.mean(wide * wide, axis=-1, keepdims=True)
        normed[block, :] = (
            wide * lax.rsqrt(square + 1e-06) * (1.0 + scale_ref[...])
        ).astype(jnp.bfloat16)
        return 0

    lax.fori_loop(0, rows // norm_rows, norm, 0)

    w_chunks = units // W_CHUNK

    def project(j, _):
        slot = j % 2
        win_copy(j, slot).wait()
        inner = jnp.dot(normed[...], win[slot], preferred_element_type=jnp.float32)
        hidden[:, pl.ds(pl.multiple_of(j * W_CHUNK, W_CHUNK), W_CHUNK)] = jax.nn.gelu(
            inner, approximate=True
        ).astype(jnp.bfloat16)

        @pl.when(j + 2 < w_chunks)
        def _():
            win_copy(j + 2, slot).start()

        return 0

    lax.fori_loop(0, w_chunks, project, 0)

    for t in range(3, half_ring + 1):
        ring_step(t)
    wown_in = wout_part(chip, 1 - core, pl.ds(0, units))
    remote(wown_in, wown_in, wown_s.at[0], wown_r.at[0], mate).wait_recv()
    for t in range(1, half_ring + 1):
        for way in range(2):
            source = ring_chip(place - t if way == 0 else place + t)
            part = wout_part(source, 1 - core, lanes_of(way, t))
            remote(part, part, cring_s.at[way, t - 1], cring_r.at[way, t - 1], mate).wait_recv()

    out_units = width // UNIT

    def terms(first, j):
        row = pl.multiple_of(first + j * UNIT, UNIT)
        return lax.dot_general(
            hidden[...], wout[pl.ds(row, UNIT), :], (((1,), (1,)), ((), ())),
            preferred_element_type=jnp.float32,
        )

    def away(j, _):
        term_out[j] = terms((1 - hid) * width, j).astype(jnp.bfloat16)
        term_copy(j).start()
        return 0

    lax.fori_loop(0, out_units, away, 0)

    def home(j, _):
        part = terms(hid * width, j)
        term_copy(j).wait_recv()
        lanes = pl.ds(pl.multiple_of(hid * width + j * UNIT, UNIT), UNIT)
        mlp = part + term_in[j].astype(jnp.float32)
        out_ref[:, pl.ds(pl.multiple_of(j * UNIT, UNIT), UNIT)] = (
            comb[:, lanes].astype(jnp.float32) + gate_ref[:, lanes] * mlp
        ).astype(jnp.bfloat16)
        return 0

    lax.fori_loop(0, out_units, home, 0)

    def sent(g, _):
        near_copy(g).wait_send()
        own_copy(g).wait_send()
        cn_copy(g).wait_send()
        x_copy(g).wait_send()

        @pl.when(has_fwd)
        def _():
            far_copy(g).wait_send()

        @pl.when(has_far)
        def _():
            cf_copy(g).wait_send()

        return 0

    lax.fori_loop(0, groups, sent, 0)
    for t in range(1, half_ring + 1):
        for way in range(2):
            ring_copy(way, t).wait_send()
            ring_mate(way, t).wait_send()
    wown_copy().wait_send()

    def term_sent(j, _):
        term_copy(j).wait_send()
        return 0

    lax.fori_loop(0, out_units, term_sent, 0)


def on_device(
    chips, queries, keys, values, residual, w_in, w_out, mod_scale, mod_gate, slot_tiles, key_tiles
):
    rows, width = queries.shape
    depth, units = w_in.shape
    groups = width // GROUP
    out_units = width // UNIT
    tile_total = slot_tiles.shape[0]
    slot = lax.axis_index("seq")
    near = (slot // 2) * 2 - 2 + jnp.arange(SLOTS, dtype=jnp.int32)
    inside = (near >= 0) & (near < tile_total)
    near_tiles = slot_tiles[jnp.clip(near, 0, tile_total - 1)]
    wanted = key_tiles[slot_tiles[slot]]
    listed = jnp.any(wanted[:, None] == near_tiles[None, :], axis=0) & inside
    bias = jnp.repeat(jnp.where(listed, 0.0, -jnp.inf).astype(jnp.float32), TILE)[None, :]

    vmem = pl.BlockSpec(memory_space=pltpu.VMEM)
    hbm = pl.BlockSpec(memory_space=pl.ANY)
    dma = pltpu.SemaphoreType.DMA
    half_ring = chips // 2
    return pl.pallas_call(
        functools.partial(block_kernel, chips),
        out_shape=jax.ShapeDtypeStruct((rows, width), jnp.bfloat16),
        in_specs=[vmem] * 5 + [hbm] * 4,
        out_specs=vmem,
        scratch_shapes=[
            pltpu.VMEM((2, SLOTS * TILE, width), jnp.bfloat16),
            pltpu.VMEM((depth, units), jnp.bfloat16),
            pltpu.VMEM((2, depth, W_CHUNK), jnp.bfloat16),
            pltpu.VMEM((rows, depth), jnp.bfloat16),
            pltpu.VMEM((rows, depth), jnp.bfloat16),
            pltpu.VMEM((rows, units), jnp.bfloat16),
            pltpu.VMEM((out_units, rows, UNIT), jnp.bfloat16),
            pltpu.VMEM((out_units, rows, UNIT), jnp.bfloat16),
            dma((3,)), dma((2,)),
        ] + [dma((groups,))] * 12 + [dma((2, half_ring))] * 4 + [dma((1,))] * 2
        + [dma((out_units,))] * 2,
        compiler_params=pltpu.CompilerParams(
            collective_id=0, has_side_effects=True, vmem_limit_bytes=62 * 1024 * 1024
        ),
    )(
        queries, residual, bias, mod_scale[None, :], mod_gate[None, :], keys, values, w_in,
        w_out.T,
    )


def solution(mesh):
    placed = (
        P("seq", "hid"),
        P("seq", "hid"),
        P("seq", "hid"),
        P("seq", "hid"),
        P(None, "hid"),
        P("hid", "seq"),
        P(),
        P(),
        P(),
        P(),
    )
    return jax.shard_map(
        functools.partial(on_device, mesh.shape["seq"] // 2),
        mesh=mesh, in_specs=placed, out_specs=P("seq", "hid"), check_vma=False,
    )
```

```python
import functools
import math

import jax
import jax.numpy as jnp
from jax import lax
from jax.experimental import pallas as pl
from jax.experimental.pallas import tpu as pltpu
from jax.sharding import PartitionSpec as P

HEAD_DIM = 128
TILE = 384
SLOTS = 6
GROUP = 256
W_CHUNK = 512
UNIT = 384
RING_GROUPS = (1, 2, 4, 5)
RING_CHUNK = 2
MESH = pl.DeviceIdType.MESH


def block_kernel(
    chips,
    q_ref, res_ref, scale_ref, gate_ref, slot_ref, list_ref, k_hbm, v_hbm, win_hbm, wout_hbm,
    out_ref,
    kv, wout, win, comb, normed, hidden, term_out, term_in, term_home, bias_ref,
    local_sem, win_sem, near_s, near_r, far_s, far_r, own_s, own_r, cn_s, cn_r, cf_s, cf_r,
    x_s, x_r, ring_s, ring_r, cring_s, cring_r, wown_s, wown_r, term_s, term_r,
):
    seq = lax.axis_index("seq")
    hid = lax.axis_index("hid")
    chip, core = seq // 2, seq % 2
    odd = chip % 2
    rows, width = q_ref.shape
    depth = win_hbm.shape[0]
    units = win_hbm.shape[1]
    groups = width // GROUP
    w_rows = wout_hbm.shape[0]
    half_ring = chips // 2
    last = 2 * (half_ring - 1)
    by_arrival = 2 * w_rows == UNIT

    def at(chip_index, core_index):
        return {"seq": chip_index * 2 + core_index}

    mate = at(chip, 1 - core)
    near = at(chip + 1 - 2 * odd, core)
    step = 2 - 4 * odd
    has_far = (chip - step >= 0) & (chip - step < chips)
    has_fwd = (chip + step >= 0) & (chip + step < chips)
    ahead = at(chip + step, core)
    behind = at(chip - step, core)
    peer = {"hid": 1 - hid}

    place = jnp.where(odd == 0, chip // 2, chips - 1 - chip // 2)

    def ring_chip(position):
        position = (position + 2 * chips) % chips
        return jnp.where(position < half_ring, 2 * position, 2 * (chips - 1 - position) + 1)

    ring_next = at(ring_chip(place + 1), core)
    ring_prev = at(ring_chip(place - 1), core)

    near_row = (4 - 4 * odd) * TILE
    far_row = 4 * odd * TILE
    mid_row = 2 * TILE

    def kv_rows(base, which):
        return pl.ds(pl.multiple_of(base + which * TILE, TILE), TILE)

    def cols(g):
        return pl.ds(pl.multiple_of(g * GROUP, GROUP), GROUP)

    def remote(src, dst, send, recv, device):
        return pltpu.make_async_remote_copy(
            src_ref=src, dst_ref=dst, send_sem=send, recv_sem=recv,
            device_id=device, device_id_type=MESH,
        )

    def mine(g):
        return kv.at[:, kv_rows(mid_row, core), cols(g)]

    def near_copy(g):
        return remote(
            mine(g), kv.at[:, kv_rows(far_row, core), cols(g)], near_s.at[g], near_r.at[g], near
        )

    def far_copy(g):
        return remote(
            kv.at[:, kv_rows(near_row, core), cols(g)],
            kv.at[:, kv_rows(far_row, core), cols(g)], far_s.at[g], far_r.at[g], ahead,
        )

    def mate_copy(base, send, recv, g):
        part = kv.at[:, kv_rows(base, core), cols(g)]
        return remote(part, part, send.at[g], recv.at[g], mate)

    def own_copy(g):
        return mate_copy(mid_row, own_s, own_r, g)

    def cn_copy(g):
        return mate_copy(near_row, cn_s, cn_r, g)

    def cf_copy(g):
        return mate_copy(far_row, cf_s, cf_r, g)

    def comb_cols(g):
        return pl.ds(pl.multiple_of(hid * width + g * GROUP, GROUP), GROUP)

    def x_copy(g):
        part = comb.at[:, comb_cols(g)]
        return remote(part, part, x_s.at[g], x_r.at[g], peer)

    def wout_part(chip_index, core_index, lanes):
        row = pl.multiple_of((chip_index * 2 + core_index) * w_rows, w_rows)
        return wout.at[pl.ds(row, w_rows), lanes]

    def ring_part(way, s, away, core_index):
        half = way if s == last else s % 2
        source = ring_chip(place - away if way == 0 else place + away)
        return wout_part(source, core_index, pl.ds(half * (units // 2), units // 2))

    def ring_copy(way, s):
        part = ring_part(way, s, s // 2, core)
        return remote(
            part, part, ring_s.at[way, s], ring_r.at[way, s],
            ring_next if way == 0 else ring_prev,
        )

    def ring_mate(way, s, core_index):
        part = ring_part(way, s, s // 2 + 1, core_index)
        return remote(part, part, cring_s.at[way, s], cring_r.at[way, s], mate)

    def ring_step(s):
        for way in range(2):
            ring_copy(way, s).wait_recv()
            if s + 2 < last:
                ring_copy(way, s + 2).start()
            elif s < last and s % 2 == way:
                ring_copy(way, last).start()
            ring_mate(way, s, core).start()

    def wown_copy():
        part = wout_part(chip, core, pl.ds(0, units))
        return remote(part, part, wown_s.at[0], wown_r.at[0], mate)

    def win_copy(j, slot):
        return pltpu.make_async_copy(
            win_hbm.at[:, pl.ds(pl.multiple_of(j * W_CHUNK, W_CHUNK), W_CHUNK)],
            win.at[slot], win_sem.at[slot],
        )

    def term_copy(j):
        return remote(term_out.at[j], term_in.at[j], term_s.at[j], term_r.at[j], peer)

    loads = [
        pltpu.make_async_copy(k_hbm, kv.at[0, kv_rows(mid_row, core), :], local_sem.at[0]),
        pltpu.make_async_copy(v_hbm, kv.at[1, kv_rows(mid_row, core), :], local_sem.at[1]),
        pltpu.make_async_copy(
            wout_hbm, wout_part(chip, core, pl.ds(0, units)), local_sem.at[2]
        ),
    ]
    for load in loads:
        load.start()
    win_copy(0, 0).start()
    win_copy(1, 1).start()

    barrier = pltpu.get_barrier_semaphore()
    for device in (mate, near, peer, ring_next, ring_prev):
        pl.semaphore_signal(barrier, inc=1, device_id=device, device_id_type=MESH)

    @pl.when(has_fwd)
    def _():
        pl.semaphore_signal(barrier, inc=1, device_id=ahead, device_id_type=MESH)

    @pl.when(has_far)
    def _():
        pl.semaphore_signal(barrier, inc=1, device_id=behind, device_id_type=MESH)

    pl.semaphore_wait(barrier, 5 + has_fwd.astype(jnp.int32) + has_far.astype(jnp.int32))

    loads[0].wait()
    loads[1].wait()

    def send_own(g, _):
        near_copy(g).start()
        own_copy(g).start()
        return 0

    lax.fori_loop(0, groups, send_own, 0)
    loads[2].wait()
    for s in range(2):
        ring_copy(0, s).start()
        ring_copy(1, s).start()
    wown_copy().start()

    tiles = slot_ref.shape[0]
    own_tile = slot_ref[seq]
    for i in range(SLOTS):
        slot = 2 * chip - 2 + i
        inside = ((slot >= 0) & (slot < tiles)).astype(jnp.int32)
        tile = slot_ref[jnp.clip(slot, 0, tiles - 1)]
        hits = jnp.int32(0)
        for j in range(list_ref.shape[1]):
            hits = hits + (list_ref[own_tile, j] == tile).astype(jnp.int32)
        bias_ref[:, i * TILE : (i + 1) * TILE] = jnp.where(
            jnp.full((1, TILE), hits * inside) > 0, 0.0, -jnp.inf
        ).astype(jnp.float32)

    @pl.when(jnp.logical_not(has_far))
    def _():
        kv[:, pl.ds(pl.multiple_of(far_row, TILE), 2 * TILE), :] = jnp.zeros(
            (2, 2 * TILE, width), kv.dtype
        )

    def attend(g):
        def head(h, _):
            lanes = pl.ds(pl.multiple_of(g * GROUP + h * HEAD_DIM, HEAD_DIM), HEAD_DIM)
            scores = lax.dot_general(
                q_ref[:, lanes], kv[0, :, lanes], (((1,), (1,)), ((), ())),
                preferred_element_type=jnp.float32,
            )
            scores = scores * (1.0 / math.sqrt(HEAD_DIM)) + bias_ref[...]
            probs = jnp.exp(scores - jnp.max(scores, axis=-1, keepdims=True))
            total = jnp.sum(probs, axis=-1, keepdims=True)
            mixed = jnp.dot(
                probs.astype(jnp.bfloat16), kv[1, :, lanes], preferred_element_type=jnp.float32
            )
            attn = (mixed / total).astype(jnp.bfloat16)
            summed = res_ref[:, lanes].astype(jnp.float32) + attn.astype(jnp.float32)
            lanes_to = pl.ds(
                pl.multiple_of(hid * width + g * GROUP + h * HEAD_DIM, HEAD_DIM), HEAD_DIM
            )
            comb[:, lanes_to] = summed.astype(jnp.bfloat16)
            return 0

        lax.fori_loop(0, GROUP // HEAD_DIM, head, 0)

    def group_step(g, _):
        @pl.when(g < groups)
        def _():
            near_in = remote(
                mine(g), kv.at[:, kv_rows(near_row, core), cols(g)], near_s.at[g], near_r.at[g],
                near,
            )
            near_in.wait_recv()

            @pl.when(has_fwd)
            def _():
                far_copy(g).start()

            cn_copy(g).start()

        @pl.when(g >= 1)
        def _():
            prior = g - 1

            @pl.when(has_far)
            def _():
                far_copy(prior).wait_recv()
                cf_copy(prior).start()

            mate_in(own_r, mid_row, prior).wait_recv()
            mate_in(cn_r, near_row, prior).wait_recv()

            @pl.when(has_far)
            def _():
                mate_in(cf_r, far_row, prior).wait_recv()

            attend(prior)
            x_copy(prior).start()

        for s, when in enumerate(RING_GROUPS):
            @pl.when(g == when)
            def _(s=s):
                ring_step(s)

        return 0

    def mate_in(recv, base, g):
        part = kv.at[:, kv_rows(base, 1 - core), cols(g)]
        return remote(part, part, own_s.at[g], recv.at[g], mate)

    lax.fori_loop(0, groups + 1, group_step, 0)

    def x_in(g, _):
        part = comb.at[:, pl.ds(pl.multiple_of((1 - hid) * width + g * GROUP, GROUP), GROUP)]
        remote(part, part, x_s.at[g], x_r.at[g], peer).wait_recv()
        return 0

    lax.fori_loop(0, groups, x_in, 0)

    norm_rows = 64

    def norm(i, _):
        block = pl.ds(pl.multiple_of(i * norm_rows, norm_rows), norm_rows)
        wide = comb[block, :].astype(jnp.float32)
        square = jnp.mean(wide * wide, axis=-1, keepdims=True)
        normed[block, :] = (
            wide * lax.rsqrt(square + 1e-06) * (1.0 + scale_ref[...])
        ).astype(jnp.bfloat16)
        return 0

    lax.fori_loop(0, rows // norm_rows, norm, 0)

    w_chunks = units // W_CHUNK

    def project(j, _):
        slot = j % 2
        win_copy(j, slot).wait()
        inner = jnp.dot(normed[...], win[slot], preferred_element_type=jnp.float32)
        hidden[:, pl.ds(pl.multiple_of(j * W_CHUNK, W_CHUNK), W_CHUNK)] = jax.nn.gelu(
            inner, approximate=True
        ).astype(jnp.bfloat16)

        @pl.when(j + 2 < w_chunks)
        def _():
            win_copy(j + 2, slot).start()

        @pl.when(j == RING_CHUNK)
        def _():
            ring_step(len(RING_GROUPS))

        return 0

    lax.fori_loop(0, w_chunks, project, 0)

    handled = len(RING_GROUPS) + 1
    wown_in = wout_part(chip, 1 - core, pl.ds(0, units))

    def arrived(t):
        if t == 0:
            remote(wown_in, wown_in, wown_s.at[0], wown_r.at[0], mate).wait_recv()
            return
        for s in range(2 * t - 2, min(2 * t, last + 1)):
            for way in range(2):
                ring_mate(way, s, 1 - core).wait_recv()

    out_units = width // UNIT

    def terms(first, j):
        row = pl.multiple_of(first + j * UNIT, UNIT)
        return lax.dot_general(
            hidden[...], wout[pl.ds(row, UNIT), :], (((1,), (1,)), ((), ())),
            preferred_element_type=jnp.float32,
        )

    def send_terms(j):
        term_out[j] = terms((1 - hid) * width, j).astype(jnp.bfloat16)
        term_copy(j).start()

    def finish(j):
        term_copy(j).wait_recv()
        lanes = pl.ds(pl.multiple_of(hid * width + j * UNIT, UNIT), UNIT)
        mlp = term_home[j] + term_in[j].astype(jnp.float32)
        out_ref[:, pl.ds(pl.multiple_of(j * UNIT, UNIT), UNIT)] = (
            comb[:, lanes].astype(jnp.float32) + gate_ref[:, lanes] * mlp
        ).astype(jnp.bfloat16)

    def blocks_at(t):
        if t == 0:
            return [chip]
        if t == half_ring:
            return [ring_chip(place + t)]
        return [ring_chip(place - t), ring_chip(place + t)]

    if by_arrival:
        for t in range(half_ring + 1):
            if t > 0:
                while handled < min(2 * t, last + 1):
                    ring_step(handled)
                    handled += 1
            arrived(t)
            for block in blocks_at(t):
                home = block // out_units == hid
                j = block % out_units

                @pl.when(jnp.logical_not(home))
                def _():
                    send_terms(j)

                @pl.when(home)
                def _():
                    term_home[j] = terms(hid * width, j)

            for block in blocks_at(t - 1) if t > 0 else []:
                @pl.when(block // out_units == hid)
                def _():
                    finish(block % out_units)

        for block in blocks_at(half_ring):
            @pl.when(block // out_units == hid)
            def _():
                finish(block % out_units)
    else:
        for s in range(handled, last + 1):
            ring_step(s)
        for t in range(half_ring + 1):
            arrived(t)

        def away(j, _):
            send_terms(j)
            return 0

        lax.fori_loop(0, out_units, away, 0)

        def at_home(j, _):
            term_home[j] = terms(hid * width, j)
            finish(j)
            return 0

        lax.fori_loop(0, out_units, at_home, 0)

    def sent(g, _):
        near_copy(g).wait_send()
        own_copy(g).wait_send()
        cn_copy(g).wait_send()
        x_copy(g).wait_send()

        @pl.when(has_fwd)
        def _():
            far_copy(g).wait_send()

        @pl.when(has_far)
        def _():
            cf_copy(g).wait_send()

        return 0

    lax.fori_loop(0, groups, sent, 0)
    for s in range(last + 1):
        for way in range(2):
            ring_copy(way, s).wait_send()
            ring_mate(way, s, core).wait_send()
    wown_copy().wait_send()

    def term_sent(j, _):
        term_copy(j).wait_send()
        return 0

    lax.fori_loop(0, out_units, term_sent, 0)


def on_device(
    chips, queries, keys, values, residual, w_in, w_out, mod_scale, mod_gate, slot_tiles, key_tiles
):
    rows, width = queries.shape
    depth, units = w_in.shape
    groups = width // GROUP
    out_units = width // UNIT
    vmem = pl.BlockSpec(memory_space=pltpu.VMEM)
    smem = pl.BlockSpec(memory_space=pltpu.SMEM)
    hbm = pl.BlockSpec(memory_space=pl.ANY)
    dma = pltpu.SemaphoreType.DMA
    half_ring = chips // 2
    return pl.pallas_call(
        functools.partial(block_kernel, chips),
        out_shape=jax.ShapeDtypeStruct((rows, width), jnp.bfloat16),
        in_specs=[vmem] * 4 + [smem] * 2 + [hbm] * 4,
        out_specs=vmem,
        scratch_shapes=[
            pltpu.VMEM((2, SLOTS * TILE, width), jnp.bfloat16),
            pltpu.VMEM((depth, units), jnp.bfloat16),
            pltpu.VMEM((2, depth, W_CHUNK), jnp.bfloat16),
            pltpu.VMEM((rows, depth), jnp.bfloat16),
            pltpu.VMEM((rows, depth), jnp.bfloat16),
            pltpu.VMEM((rows, units), jnp.bfloat16),
            pltpu.VMEM((out_units, rows, UNIT), jnp.bfloat16),
            pltpu.VMEM((out_units, rows, UNIT), jnp.bfloat16),
            pltpu.VMEM((out_units, rows, UNIT), jnp.float32),
            pltpu.VMEM((1, SLOTS * TILE), jnp.float32),
            dma((3,)), dma((2,)),
        ] + [dma((groups,))] * 12 + [dma((2, 2 * half_ring - 1))] * 4 + [dma((1,))] * 2
        + [dma((out_units,))] * 2,
        compiler_params=pltpu.CompilerParams(
            collective_id=0, has_side_effects=True, vmem_limit_bytes=62 * 1024 * 1024
        ),
    )(
        queries, residual, mod_scale[None, :], mod_gate[None, :], slot_tiles, key_tiles,
        keys, values, w_in, w_out.T,
    )


def solution(mesh):
    placed = (
        P("seq", "hid"),
        P("seq", "hid"),
        P("seq", "hid"),
        P("seq", "hid"),
        P(None, "hid"),
        P("hid", "seq"),
        P(),
        P(),
        P(),
        P(),
    )
    return jax.shard_map(
        functools.partial(on_device, mesh.shape["seq"] // 2),
        mesh=mesh, in_specs=placed, out_specs=P("seq", "hid"), check_vma=False,
    )
```

```python
import functools
import math

import jax
import jax.numpy as jnp
from jax import lax
from jax.experimental import pallas as pl
from jax.experimental.pallas import tpu as pltpu
from jax.sharding import PartitionSpec as P

HEAD_DIM = 128
TILE = 384
SLOTS = 6
GROUP = 256
W_CHUNK = 512
UNIT = 384
PASS_GROUPS = (3, 5)
PASS_CHUNK = 2
MESH = pl.DeviceIdType.MESH


def block_kernel(
    chips,
    q_ref, res_ref, scale_ref, gate_ref, slot_ref, list_ref, k_hbm, v_hbm, win_hbm, wout_hbm,
    out_ref,
    kv, wout, win, comb, normed, hidden, term_out, term_in, term_home, bias_ref,
    local_sem, win_sem, near_s, near_r, far_s, far_r, own_s, own_r, cn_s, cn_r, cf_s, cf_r,
    x_s, x_r, up_s, up_r, over_s, over_r, cup_s, cup_r, cover_s, cover_r, wown_s, wown_r,
    term_s, term_r,
):
    seq = lax.axis_index("seq")
    hid = lax.axis_index("hid")
    chip, core = seq // 2, seq % 2
    odd = chip % 2
    rows, width = q_ref.shape
    depth = win_hbm.shape[0]
    units = win_hbm.shape[1]
    groups = width // GROUP
    w_rows = wout_hbm.shape[0]
    column = chips // 2
    by_arrival = 2 * w_rows == UNIT

    def at(chip_index, core_index):
        return {"seq": chip_index * 2 + core_index}

    mate = at(chip, 1 - core)
    near = at(chip + 1 - 2 * odd, core)
    step = 2 - 4 * odd
    has_far = (chip - step >= 0) & (chip - step < chips)
    has_fwd = (chip + step >= 0) & (chip + step < chips)
    ahead = at(chip + step, core)
    behind = at(chip - step, core)
    peer = {"hid": 1 - hid}

    place = chip // 2

    def member(i, parity):
        other = place
        bit = 1
        while bit <= i:
            if i & bit:
                other = other + bit - 2 * bit * ((place // bit) % 2)
            bit *= 2
        return 2 * other + parity

    near_row = (4 - 4 * odd) * TILE
    far_row = 4 * odd * TILE
    mid_row = 2 * TILE

    def kv_rows(base, which):
        return pl.ds(pl.multiple_of(base + which * TILE, TILE), TILE)

    def cols(g):
        return pl.ds(pl.multiple_of(g * GROUP, GROUP), GROUP)

    def remote(src, dst, send, recv, device):
        return pltpu.make_async_remote_copy(
            src_ref=src, dst_ref=dst, send_sem=send, recv_sem=recv,
            device_id=device, device_id_type=MESH,
        )

    def mine(g):
        return kv.at[:, kv_rows(mid_row, core), cols(g)]

    def near_copy(g):
        return remote(
            mine(g), kv.at[:, kv_rows(far_row, core), cols(g)], near_s.at[g], near_r.at[g], near
        )

    def far_copy(g):
        return remote(
            kv.at[:, kv_rows(near_row, core), cols(g)],
            kv.at[:, kv_rows(far_row, core), cols(g)], far_s.at[g], far_r.at[g], ahead,
        )

    def mate_copy(base, send, recv, g):
        part = kv.at[:, kv_rows(base, core), cols(g)]
        return remote(part, part, send.at[g], recv.at[g], mate)

    def own_copy(g):
        return mate_copy(mid_row, own_s, own_r, g)

    def cn_copy(g):
        return mate_copy(near_row, cn_s, cn_r, g)

    def cf_copy(g):
        return mate_copy(far_row, cf_s, cf_r, g)

    def comb_cols(g):
        return pl.ds(pl.multiple_of(hid * width + g * GROUP, GROUP), GROUP)

    def x_copy(g):
        part = comb.at[:, comb_cols(g)]
        return remote(part, part, x_s.at[g], x_r.at[g], peer)

    def wout_part(chip_index, core_index, lanes):
        row = pl.multiple_of((chip_index * 2 + core_index) * w_rows, w_rows)
        return wout.at[pl.ds(row, w_rows), lanes]

    every = pl.ds(0, units)

    def up_copy(i):
        part = wout_part(chip, core, every)
        return remote(part, part, up_s.at[i], up_r.at[i], at(member(i, odd), core))

    def up_in(i):
        part = wout_part(member(i, odd), core, every)
        return remote(part, part, up_s.at[i], up_r.at[i], at(member(i, odd), core))

    def over_copy(i):
        part = wout_part(member(i, odd), core, every)
        return remote(part, part, over_s.at[i], over_r.at[i], near)

    def over_in(i):
        part = wout_part(member(i, 1 - odd), core, every)
        return remote(part, part, over_s.at[i], over_r.at[i], near)

    def up_mate(i, core_index):
        part = wout_part(member(i, odd), core_index, every)
        return remote(part, part, cup_s.at[i], cup_r.at[i], mate)

    def over_mate(i, core_index):
        part = wout_part(member(i, 1 - odd), core_index, every)
        return remote(part, part, cover_s.at[i], cover_r.at[i], mate)

    def pass_up(i):
        up_in(i).wait_recv()
        over_copy(i).start()
        up_mate(i, core).start()

    def pass_over(i):
        over_in(i).wait_recv()
        over_mate(i, core).start()

    def wown_copy():
        part = wout_part(chip, core, pl.ds(0, units))
        return remote(part, part, wown_s.at[0], wown_r.at[0], mate)

    def win_copy(j, slot):
        return pltpu.make_async_copy(
            win_hbm.at[:, pl.ds(pl.multiple_of(j * W_CHUNK, W_CHUNK), W_CHUNK)],
            win.at[slot], win_sem.at[slot],
        )

    def term_copy(j):
        return remote(term_out.at[j], term_in.at[j], term_s.at[j], term_r.at[j], peer)

    loads = [
        pltpu.make_async_copy(k_hbm, kv.at[0, kv_rows(mid_row, core), :], local_sem.at[0]),
        pltpu.make_async_copy(v_hbm, kv.at[1, kv_rows(mid_row, core), :], local_sem.at[1]),
        pltpu.make_async_copy(
            wout_hbm, wout_part(chip, core, pl.ds(0, units)), local_sem.at[2]
        ),
    ]
    for load in loads:
        load.start()
    win_copy(0, 0).start()
    win_copy(1, 1).start()

    barrier = pltpu.get_barrier_semaphore()
    members = [at(member(i, odd), core) for i in range(1, column)]
    for device in [mate, near, peer] + members:
        pl.semaphore_signal(barrier, inc=1, device_id=device, device_id_type=MESH)

    @pl.when(has_fwd)
    def _():
        pl.semaphore_signal(barrier, inc=1, device_id=ahead, device_id_type=MESH)

    @pl.when(has_far)
    def _():
        pl.semaphore_signal(barrier, inc=1, device_id=behind, device_id_type=MESH)

    pl.semaphore_wait(barrier, column + 2 + has_fwd.astype(jnp.int32) + has_far.astype(jnp.int32))

    loads[0].wait()
    loads[1].wait()

    def send_own(g, _):
        near_copy(g).start()
        own_copy(g).start()
        return 0

    lax.fori_loop(0, 2, send_own, 0)
    loads[2].wait()
    up_copy(1).start()
    lax.fori_loop(2, 4, send_own, 0)
    for i in range(2, column):
        up_copy(i).start()
    lax.fori_loop(4, groups, send_own, 0)
    over_copy(0).start()
    wown_copy().start()

    tiles = slot_ref.shape[0]
    own_tile = slot_ref[seq]
    for i in range(SLOTS):
        slot = 2 * chip - 2 + i
        inside = ((slot >= 0) & (slot < tiles)).astype(jnp.int32)
        tile = slot_ref[jnp.clip(slot, 0, tiles - 1)]
        hits = jnp.int32(0)
        for j in range(list_ref.shape[1]):
            hits = hits + (list_ref[own_tile, j] == tile).astype(jnp.int32)
        bias_ref[:, i * TILE : (i + 1) * TILE] = jnp.where(
            jnp.full((1, TILE), hits * inside) > 0, 0.0, -jnp.inf
        ).astype(jnp.float32)

    @pl.when(jnp.logical_not(has_far))
    def _():
        kv[:, pl.ds(pl.multiple_of(far_row, TILE), 2 * TILE), :] = jnp.zeros(
            (2, 2 * TILE, width), kv.dtype
        )

    def attend(g):
        def head(h, _):
            lanes = pl.ds(pl.multiple_of(g * GROUP + h * HEAD_DIM, HEAD_DIM), HEAD_DIM)
            scores = lax.dot_general(
                q_ref[:, lanes], kv[0, :, lanes], (((1,), (1,)), ((), ())),
                preferred_element_type=jnp.float32,
            )
            scores = scores * (1.0 / math.sqrt(HEAD_DIM)) + bias_ref[...]
            probs = jnp.exp(scores - jnp.max(scores, axis=-1, keepdims=True))
            total = jnp.sum(probs, axis=-1, keepdims=True)
            mixed = jnp.dot(
                probs.astype(jnp.bfloat16), kv[1, :, lanes], preferred_element_type=jnp.float32
            )
            attn = (mixed / total).astype(jnp.bfloat16)
            summed = res_ref[:, lanes].astype(jnp.float32) + attn.astype(jnp.float32)
            lanes_to = pl.ds(
                pl.multiple_of(hid * width + g * GROUP + h * HEAD_DIM, HEAD_DIM), HEAD_DIM
            )
            comb[:, lanes_to] = summed.astype(jnp.bfloat16)
            return 0

        lax.fori_loop(0, GROUP // HEAD_DIM, head, 0)

    def group_step(g, _):
        @pl.when(g < groups)
        def _():
            near_in = remote(
                mine(g), kv.at[:, kv_rows(near_row, core), cols(g)], near_s.at[g], near_r.at[g],
                near,
            )
            near_in.wait_recv()

            @pl.when(has_fwd)
            def _():
                far_copy(g).start()

            cn_copy(g).start()

        @pl.when(g >= 1)
        def _():
            prior = g - 1

            @pl.when(has_far)
            def _():
                far_copy(prior).wait_recv()
                cf_copy(prior).start()

            mate_in(own_r, mid_row, prior).wait_recv()
            mate_in(cn_r, near_row, prior).wait_recv()

            @pl.when(has_far)
            def _():
                mate_in(cf_r, far_row, prior).wait_recv()

            attend(prior)
            x_copy(prior).start()

        for i, when in enumerate(PASS_GROUPS):
            @pl.when(g == when)
            def _():
                pass_up(i + 1)

        return 0

    def mate_in(recv, base, g):
        part = kv.at[:, kv_rows(base, 1 - core), cols(g)]
        return remote(part, part, own_s.at[g], recv.at[g], mate)

    lax.fori_loop(0, groups + 1, group_step, 0)
    for i in range(len(PASS_GROUPS) + 1, column):
        pass_up(i)
    pass_over(0)

    def x_in(g, _):
        part = comb.at[:, pl.ds(pl.multiple_of((1 - hid) * width + g * GROUP, GROUP), GROUP)]
        remote(part, part, x_s.at[g], x_r.at[g], peer).wait_recv()
        return 0

    lax.fori_loop(0, groups, x_in, 0)

    norm_rows = 64

    def norm(i, _):
        block = pl.ds(pl.multiple_of(i * norm_rows, norm_rows), norm_rows)
        wide = comb[block, :].astype(jnp.float32)
        square = jnp.mean(wide * wide, axis=-1, keepdims=True)
        normed[block, :] = (
            wide * lax.rsqrt(square + 1e-06) * (1.0 + scale_ref[...])
        ).astype(jnp.bfloat16)
        return 0

    lax.fori_loop(0, rows // norm_rows, norm, 0)

    w_chunks = units // W_CHUNK

    def project(j, _):
        slot = j % 2
        win_copy(j, slot).wait()
        inner = jnp.dot(normed[...], win[slot], preferred_element_type=jnp.float32)
        hidden[:, pl.ds(pl.multiple_of(j * W_CHUNK, W_CHUNK), W_CHUNK)] = jax.nn.gelu(
            inner, approximate=True
        ).astype(jnp.bfloat16)

        @pl.when(j + 2 < w_chunks)
        def _():
            win_copy(j + 2, slot).start()

        @pl.when(j == PASS_CHUNK)
        def _():
            pass_over(1)

        return 0

    lax.fori_loop(0, w_chunks, project, 0)

    wown_in = wout_part(chip, 1 - core, every)

    def own_arrived():
        remote(wown_in, wown_in, wown_s.at[0], wown_r.at[0], mate).wait_recv()

    def up_arrived(i):
        up_mate(i, 1 - core).wait_recv()

    def over_arrived(i):
        if i >= 2:
            pass_over(i)
        over_mate(i, 1 - core).wait_recv()

    order = [(own_arrived, chip)]
    order += [(functools.partial(up_arrived, i), member(i, odd)) for i in range(1, column)]
    order += [(functools.partial(over_arrived, i), member(i, 1 - odd)) for i in range(column)]

    out_units = width // UNIT

    def terms(first, j):
        row = pl.multiple_of(first + j * UNIT, UNIT)
        return lax.dot_general(
            hidden[...], wout[pl.ds(row, UNIT), :], (((1,), (1,)), ((), ())),
            preferred_element_type=jnp.float32,
        )

    def send_terms(j):
        term_out[j] = terms((1 - hid) * width, j).astype(jnp.bfloat16)
        term_copy(j).start()

    def finish(j):
        term_copy(j).wait_recv()
        lanes = pl.ds(pl.multiple_of(hid * width + j * UNIT, UNIT), UNIT)
        mlp = term_home[j] + term_in[j].astype(jnp.float32)
        out_ref[:, pl.ds(pl.multiple_of(j * UNIT, UNIT), UNIT)] = (
            comb[:, lanes].astype(jnp.float32) + gate_ref[:, lanes] * mlp
        ).astype(jnp.bfloat16)

    def finish_block(block):
        @pl.when(block // out_units == hid)
        def _():
            finish(block % out_units)

    if by_arrival:
        for n, (arrived, block) in enumerate(order):
            arrived()

            @pl.when(block // out_units != hid)
            def _():
                send_terms(block % out_units)

            @pl.when(block // out_units == hid)
            def _():
                term_home[block % out_units] = terms(hid * width, block % out_units)

            if n > 0:
                finish_block(order[n - 1][1])
        finish_block(order[-1][1])
    else:
        for arrived, _ in order:
            arrived()

        def away(j, _):
            send_terms(j)
            return 0

        lax.fori_loop(0, out_units, away, 0)

        def at_home(j, _):
            term_home[j] = terms(hid * width, j)
            finish(j)
            return 0

        lax.fori_loop(0, out_units, at_home, 0)

    def sent(g, _):
        near_copy(g).wait_send()
        own_copy(g).wait_send()
        cn_copy(g).wait_send()
        x_copy(g).wait_send()

        @pl.when(has_fwd)
        def _():
            far_copy(g).wait_send()

        @pl.when(has_far)
        def _():
            cf_copy(g).wait_send()

        return 0

    lax.fori_loop(0, groups, sent, 0)
    for i in range(column):
        over_copy(i).wait_send()
        over_mate(i, core).wait_send()
        if i > 0:
            up_copy(i).wait_send()
            up_mate(i, core).wait_send()
    wown_copy().wait_send()

    def term_sent(j, _):
        term_copy(j).wait_send()
        return 0

    lax.fori_loop(0, out_units, term_sent, 0)


def on_device(
    chips, queries, keys, values, residual, w_in, w_out, mod_scale, mod_gate, slot_tiles, key_tiles
):
    rows, width = queries.shape
    depth, units = w_in.shape
    groups = width // GROUP
    out_units = width // UNIT
    vmem = pl.BlockSpec(memory_space=pltpu.VMEM)
    smem = pl.BlockSpec(memory_space=pltpu.SMEM)
    hbm = pl.BlockSpec(memory_space=pl.ANY)
    dma = pltpu.SemaphoreType.DMA
    column = chips // 2
    return pl.pallas_call(
        functools.partial(block_kernel, chips),
        out_shape=jax.ShapeDtypeStruct((rows, width), jnp.bfloat16),
        in_specs=[vmem] * 4 + [smem] * 2 + [hbm] * 4,
        out_specs=vmem,
        scratch_shapes=[
            pltpu.VMEM((2, SLOTS * TILE, width), jnp.bfloat16),
            pltpu.VMEM((depth, units), jnp.bfloat16),
            pltpu.VMEM((2, depth, W_CHUNK), jnp.bfloat16),
            pltpu.VMEM((rows, depth), jnp.bfloat16),
            pltpu.VMEM((rows, depth), jnp.bfloat16),
            pltpu.VMEM((rows, units), jnp.bfloat16),
            pltpu.VMEM((out_units, rows, UNIT), jnp.bfloat16),
            pltpu.VMEM((out_units, rows, UNIT), jnp.bfloat16),
            pltpu.VMEM((out_units, rows, UNIT), jnp.float32),
            pltpu.VMEM((1, SLOTS * TILE), jnp.float32),
            dma((3,)), dma((2,)),
        ] + [dma((groups,))] * 12 + [dma((column,))] * 8 + [dma((1,))] * 2
        + [dma((out_units,))] * 2,
        compiler_params=pltpu.CompilerParams(
            collective_id=0, has_side_effects=True, vmem_limit_bytes=62 * 1024 * 1024
        ),
    )(
        queries, residual, mod_scale[None, :], mod_gate[None, :], slot_tiles, key_tiles,
        keys, values, w_in, w_out.T,
    )


def solution(mesh):
    placed = (
        P("seq", "hid"),
        P("seq", "hid"),
        P("seq", "hid"),
        P("seq", "hid"),
        P(None, "hid"),
        P("hid", "seq"),
        P(),
        P(),
        P(),
        P(),
    )
    return jax.shard_map(
        functools.partial(on_device, mesh.shape["seq"] // 2),
        mesh=mesh, in_specs=placed, out_specs=P("seq", "hid"), check_vma=False,
    )
```

```python
import functools
import math

import jax
import jax.numpy as jnp
from jax import lax
from jax.experimental import pallas as pl
from jax.experimental.pallas import tpu as pltpu
from jax.sharding import PartitionSpec as P

HEAD_DIM = 128
TILE = 384
SLOTS = 6
GROUP = 256
W_CHUNK = 512
UNIT = 384
RING_START = 4
RING_GROUPS = (6,)
RING_CHUNKS = (0, 2, 5)
MESH = pl.DeviceIdType.MESH


def block_kernel(
    chips,
    q_ref, res_ref, scale_ref, gate_ref, slot_ref, list_ref, k_hbm, v_hbm, win_hbm, wout_hbm,
    out_ref,
    kv, wout, win, comb, normed, hidden, term_out, term_in, term_home, bias_ref,
    local_sem, win_sem, near_s, near_r, far_s, far_r, own_s, own_r, cn_s, cn_r, cf_s, cf_r,
    x_s, x_r, ring_s, ring_r, cring_s, cring_r, wown_s, wown_r, term_s, term_r,
):
    seq = lax.axis_index("seq")
    hid = lax.axis_index("hid")
    chip, core = seq // 2, seq % 2
    odd = chip % 2
    rows, width = q_ref.shape
    depth = win_hbm.shape[0]
    units = win_hbm.shape[1]
    groups = width // GROUP
    w_rows = wout_hbm.shape[0]
    half_ring = chips // 2
    last = 2 * (half_ring - 1)
    by_arrival = 2 * w_rows == UNIT

    def at(chip_index, core_index):
        return {"seq": chip_index * 2 + core_index}

    mate = at(chip, 1 - core)
    near = at(chip + 1 - 2 * odd, core)
    step = 2 - 4 * odd
    has_far = (chip - step >= 0) & (chip - step < chips)
    has_fwd = (chip + step >= 0) & (chip + step < chips)
    ahead = at(chip + step, core)
    behind = at(chip - step, core)
    peer = {"hid": 1 - hid}

    place = jnp.where(odd == 0, chip // 2, chips - 1 - chip // 2)

    def ring_chip(position):
        position = (position + 2 * chips) % chips
        return jnp.where(position < half_ring, 2 * position, 2 * (chips - 1 - position) + 1)

    ring_next = at(ring_chip(place + 1), core)
    ring_prev = at(ring_chip(place - 1), core)

    near_row = (4 - 4 * odd) * TILE
    far_row = 4 * odd * TILE
    mid_row = 2 * TILE

    def kv_rows(base, which):
        return pl.ds(pl.multiple_of(base + which * TILE, TILE), TILE)

    def cols(g):
        return pl.ds(pl.multiple_of(g * GROUP, GROUP), GROUP)

    def remote(src, dst, send, recv, device):
        return pltpu.make_async_remote_copy(
            src_ref=src, dst_ref=dst, send_sem=send, recv_sem=recv,
            device_id=device, device_id_type=MESH,
        )

    def mine(g):
        return kv.at[:, kv_rows(mid_row, core), cols(g)]

    def near_copy(g):
        return remote(
            mine(g), kv.at[:, kv_rows(far_row, core), cols(g)], near_s.at[g], near_r.at[g], near
        )

    def far_copy(g):
        return remote(
            kv.at[:, kv_rows(near_row, core), cols(g)],
            kv.at[:, kv_rows(far_row, core), cols(g)], far_s.at[g], far_r.at[g], ahead,
        )

    def mate_copy(base, send, recv, g):
        part = kv.at[:, kv_rows(base, core), cols(g)]
        return remote(part, part, send.at[g], recv.at[g], mate)

    def own_copy(g):
        return mate_copy(mid_row, own_s, own_r, g)

    def cn_copy(g):
        return mate_copy(near_row, cn_s, cn_r, g)

    def cf_copy(g):
        return mate_copy(far_row, cf_s, cf_r, g)

    def comb_cols(g):
        return pl.ds(pl.multiple_of(hid * width + g * GROUP, GROUP), GROUP)

    def x_copy(g):
        part = comb.at[:, comb_cols(g)]
        return remote(part, part, x_s.at[g], x_r.at[g], peer)

    def wout_part(chip_index, core_index, lanes):
        row = pl.multiple_of((chip_index * 2 + core_index) * w_rows, w_rows)
        return wout.at[pl.ds(row, w_rows), lanes]

    def ring_part(way, s, away, core_index):
        half = way if s == last else s % 2
        source = ring_chip(place - away if way == 0 else place + away)
        return wout_part(source, core_index, pl.ds(half * (units // 2), units // 2))

    def ring_copy(way, s):
        part = ring_part(way, s, s // 2, core)
        return remote(
            part, part, ring_s.at[way, s], ring_r.at[way, s],
            ring_next if way == 0 else ring_prev,
        )

    def ring_mate(way, s, core_index):
        part = ring_part(way, s, s // 2 + 1, core_index)
        return remote(part, part, cring_s.at[way, s], cring_r.at[way, s], mate)

    def ring_step(s):
        for way in range(2):
            ring_copy(way, s).wait_recv()
            if s + 2 < last:
                ring_copy(way, s + 2).start()
            elif s < last and s % 2 == way:
                ring_copy(way, last).start()
            ring_mate(way, s, core).start()

    def wown_copy():
        part = wout_part(chip, core, pl.ds(0, units))
        return remote(part, part, wown_s.at[0], wown_r.at[0], mate)

    def win_copy(j, slot):
        return pltpu.make_async_copy(
            win_hbm.at[:, pl.ds(pl.multiple_of(j * W_CHUNK, W_CHUNK), W_CHUNK)],
            win.at[slot], win_sem.at[slot],
        )

    def term_copy(j):
        return remote(term_out.at[j], term_in.at[j], term_s.at[j], term_r.at[j], peer)

    loads = [
        pltpu.make_async_copy(k_hbm, kv.at[0, kv_rows(mid_row, core), :], local_sem.at[0]),
        pltpu.make_async_copy(v_hbm, kv.at[1, kv_rows(mid_row, core), :], local_sem.at[1]),
        pltpu.make_async_copy(
            wout_hbm, wout_part(chip, core, pl.ds(0, units)), local_sem.at[2]
        ),
    ]
    for load in loads:
        load.start()
    win_copy(0, 0).start()
    win_copy(1, 1).start()

    barrier = pltpu.get_barrier_semaphore()
    for device in (mate, near, peer, ring_next, ring_prev):
        pl.semaphore_signal(barrier, inc=1, device_id=device, device_id_type=MESH)

    @pl.when(has_fwd)
    def _():
        pl.semaphore_signal(barrier, inc=1, device_id=ahead, device_id_type=MESH)

    @pl.when(has_far)
    def _():
        pl.semaphore_signal(barrier, inc=1, device_id=behind, device_id_type=MESH)

    pl.semaphore_wait(barrier, 5 + has_fwd.astype(jnp.int32) + has_far.astype(jnp.int32))

    loads[0].wait()
    loads[1].wait()

    def send_own(g, _):
        near_copy(g).start()
        own_copy(g).start()
        return 0

    lax.fori_loop(0, groups, send_own, 0)
    loads[2].wait()
    wown_copy().start()

    tiles = slot_ref.shape[0]
    own_tile = slot_ref[seq]
    for i in range(SLOTS):
        slot = 2 * chip - 2 + i
        inside = ((slot >= 0) & (slot < tiles)).astype(jnp.int32)
        tile = slot_ref[jnp.clip(slot, 0, tiles - 1)]
        hits = jnp.int32(0)
        for j in range(list_ref.shape[1]):
            hits = hits + (list_ref[own_tile, j] == tile).astype(jnp.int32)
        bias_ref[:, i * TILE : (i + 1) * TILE] = jnp.where(
            jnp.full((1, TILE), hits * inside) > 0, 0.0, -jnp.inf
        ).astype(jnp.float32)

    @pl.when(jnp.logical_not(has_far))
    def _():
        kv[:, pl.ds(pl.multiple_of(far_row, TILE), 2 * TILE), :] = jnp.zeros(
            (2, 2 * TILE, width), kv.dtype
        )

    def attend(g):
        def head(h, _):
            lanes = pl.ds(pl.multiple_of(g * GROUP + h * HEAD_DIM, HEAD_DIM), HEAD_DIM)
            scores = lax.dot_general(
                q_ref[:, lanes], kv[0, :, lanes], (((1,), (1,)), ((), ())),
                preferred_element_type=jnp.float32,
            )
            scores = scores * (1.0 / math.sqrt(HEAD_DIM)) + bias_ref[...]
            probs = jnp.exp(scores - jnp.max(scores, axis=-1, keepdims=True))
            total = jnp.sum(probs, axis=-1, keepdims=True)
            mixed = jnp.dot(
                probs.astype(jnp.bfloat16), kv[1, :, lanes], preferred_element_type=jnp.float32
            )
            attn = (mixed / total).astype(jnp.bfloat16)
            summed = res_ref[:, lanes].astype(jnp.float32) + attn.astype(jnp.float32)
            lanes_to = pl.ds(
                pl.multiple_of(hid * width + g * GROUP + h * HEAD_DIM, HEAD_DIM), HEAD_DIM
            )
            comb[:, lanes_to] = summed.astype(jnp.bfloat16)
            return 0

        lax.fori_loop(0, GROUP // HEAD_DIM, head, 0)

    def group_step(g, _):
        @pl.when(g < groups)
        def _():
            near_in = remote(
                mine(g), kv.at[:, kv_rows(near_row, core), cols(g)], near_s.at[g], near_r.at[g],
                near,
            )
            near_in.wait_recv()

            @pl.when(has_fwd)
            def _():
                far_copy(g).start()

            cn_copy(g).start()

        @pl.when(g == RING_START)
        def _():
            for s in range(2):
                ring_copy(0, s).start()
                ring_copy(1, s).start()

        @pl.when(g >= 1)
        def _():
            prior = g - 1

            @pl.when(has_far)
            def _():
                far_copy(prior).wait_recv()
                cf_copy(prior).start()

            mate_in(own_r, mid_row, prior).wait_recv()
            mate_in(cn_r, near_row, prior).wait_recv()

            @pl.when(has_far)
            def _():
                mate_in(cf_r, far_row, prior).wait_recv()

            attend(prior)
            x_copy(prior).start()

        for s, when in enumerate(RING_GROUPS):
            @pl.when(g == when)
            def _(s=s):
                ring_step(s)

        return 0

    def mate_in(recv, base, g):
        part = kv.at[:, kv_rows(base, 1 - core), cols(g)]
        return remote(part, part, own_s.at[g], recv.at[g], mate)

    lax.fori_loop(0, groups + 1, group_step, 0)

    def x_in(g, _):
        part = comb.at[:, pl.ds(pl.multiple_of((1 - hid) * width + g * GROUP, GROUP), GROUP)]
        remote(part, part, x_s.at[g], x_r.at[g], peer).wait_recv()
        return 0

    lax.fori_loop(0, groups, x_in, 0)

    norm_rows = 64

    def norm(i, _):
        block = pl.ds(pl.multiple_of(i * norm_rows, norm_rows), norm_rows)
        wide = comb[block, :].astype(jnp.float32)
        square = jnp.mean(wide * wide, axis=-1, keepdims=True)
        normed[block, :] = (
            wide * lax.rsqrt(square + 1e-06) * (1.0 + scale_ref[...])
        ).astype(jnp.bfloat16)
        return 0

    lax.fori_loop(0, rows // norm_rows, norm, 0)

    w_chunks = units // W_CHUNK

    def project(j, _):
        slot = j % 2
        win_copy(j, slot).wait()
        inner = jnp.dot(normed[...], win[slot], preferred_element_type=jnp.float32)
        hidden[:, pl.ds(pl.multiple_of(j * W_CHUNK, W_CHUNK), W_CHUNK)] = jax.nn.gelu(
            inner, approximate=True
        ).astype(jnp.bfloat16)

        @pl.when(j + 2 < w_chunks)
        def _():
            win_copy(j + 2, slot).start()

        for s, when in enumerate(RING_CHUNKS):
            @pl.when(j == when)
            def _():
                ring_step(len(RING_GROUPS) + s)

        return 0

    lax.fori_loop(0, w_chunks, project, 0)

    handled = len(RING_GROUPS) + len(RING_CHUNKS)
    wown_in = wout_part(chip, 1 - core, pl.ds(0, units))

    def arrived(t):
        if t == 0:
            remote(wown_in, wown_in, wown_s.at[0], wown_r.at[0], mate).wait_recv()
            return
        for s in range(2 * t - 2, min(2 * t, last + 1)):
            for way in range(2):
                ring_mate(way, s, 1 - core).wait_recv()

    out_units = width // UNIT

    def terms(first, j):
        row = pl.multiple_of(first + j * UNIT, UNIT)
        return lax.dot_general(
            hidden[...], wout[pl.ds(row, UNIT), :], (((1,), (1,)), ((), ())),
            preferred_element_type=jnp.float32,
        )

    def send_terms(j):
        term_out[j] = terms((1 - hid) * width, j).astype(jnp.bfloat16)
        term_copy(j).start()

    def finish(j):
        term_copy(j).wait_recv()
        lanes = pl.ds(pl.multiple_of(hid * width + j * UNIT, UNIT), UNIT)
        mlp = term_home[j] + term_in[j].astype(jnp.float32)
        out_ref[:, pl.ds(pl.multiple_of(j * UNIT, UNIT), UNIT)] = (
            comb[:, lanes].astype(jnp.float32) + gate_ref[:, lanes] * mlp
        ).astype(jnp.bfloat16)

    def blocks_at(t):
        if t == 0:
            return [chip]
        if t == half_ring:
            return [ring_chip(place + t)]
        return [ring_chip(place - t), ring_chip(place + t)]

    if by_arrival:
        for t in range(half_ring + 1):
            if t > 0:
                while handled < min(2 * t, last + 1):
                    ring_step(handled)
                    handled += 1
            arrived(t)
            for block in blocks_at(t):
                home = block // out_units == hid
                j = block % out_units

                @pl.when(jnp.logical_not(home))
                def _():
                    send_terms(j)

                @pl.when(home)
                def _():
                    term_home[j] = terms(hid * width, j)

            for block in blocks_at(t - 1) if t > 0 else []:
                @pl.when(block // out_units == hid)
                def _():
                    finish(block % out_units)

        for block in blocks_at(half_ring):
            @pl.when(block // out_units == hid)
            def _():
                finish(block % out_units)
    else:
        for s in range(handled, last + 1):
            ring_step(s)
        for t in range(half_ring + 1):
            arrived(t)

        def away(j, _):
            send_terms(j)
            return 0

        lax.fori_loop(0, out_units, away, 0)

        def at_home(j, _):
            term_home[j] = terms(hid * width, j)
            finish(j)
            return 0

        lax.fori_loop(0, out_units, at_home, 0)

    def sent(g, _):
        near_copy(g).wait_send()
        own_copy(g).wait_send()
        cn_copy(g).wait_send()
        x_copy(g).wait_send()

        @pl.when(has_fwd)
        def _():
            far_copy(g).wait_send()

        @pl.when(has_far)
        def _():
            cf_copy(g).wait_send()

        return 0

    lax.fori_loop(0, groups, sent, 0)
    for s in range(last + 1):
        for way in range(2):
            ring_copy(way, s).wait_send()
            ring_mate(way, s, core).wait_send()
    wown_copy().wait_send()

    def term_sent(j, _):
        term_copy(j).wait_send()
        return 0

    lax.fori_loop(0, out_units, term_sent, 0)


def on_device(
    chips, queries, keys, values, residual, w_in, w_out, mod_scale, mod_gate, slot_tiles, key_tiles
):
    rows, width = queries.shape
    depth, units = w_in.shape
    groups = width // GROUP
    out_units = width // UNIT
    vmem = pl.BlockSpec(memory_space=pltpu.VMEM)
    smem = pl.BlockSpec(memory_space=pltpu.SMEM)
    hbm = pl.BlockSpec(memory_space=pl.ANY)
    dma = pltpu.SemaphoreType.DMA
    half_ring = chips // 2
    return pl.pallas_call(
        functools.partial(block_kernel, chips),
        out_shape=jax.ShapeDtypeStruct((rows, width), jnp.bfloat16),
        in_specs=[vmem] * 4 + [smem] * 2 + [hbm] * 4,
        out_specs=vmem,
        scratch_shapes=[
            pltpu.VMEM((2, SLOTS * TILE, width), jnp.bfloat16),
            pltpu.VMEM((depth, units), jnp.bfloat16),
            pltpu.VMEM((2, depth, W_CHUNK), jnp.bfloat16),
            pltpu.VMEM((rows, depth), jnp.bfloat16),
            pltpu.VMEM((rows, depth), jnp.bfloat16),
            pltpu.VMEM((rows, units), jnp.bfloat16),
            pltpu.VMEM((out_units, rows, UNIT), jnp.bfloat16),
            pltpu.VMEM((out_units, rows, UNIT), jnp.bfloat16),
            pltpu.VMEM((out_units, rows, UNIT), jnp.float32),
            pltpu.VMEM((1, SLOTS * TILE), jnp.float32),
            dma((3,)), dma((2,)),
        ] + [dma((groups,))] * 12 + [dma((2, 2 * half_ring - 1))] * 4 + [dma((1,))] * 2
        + [dma((out_units,))] * 2,
        compiler_params=pltpu.CompilerParams(
            collective_id=0, has_side_effects=True, vmem_limit_bytes=62 * 1024 * 1024
        ),
    )(
        queries, residual, mod_scale[None, :], mod_gate[None, :], slot_tiles, key_tiles,
        keys, values, w_in, w_out.T,
    )


def solution(mesh):
    placed = (
        P("seq", "hid"),
        P("seq", "hid"),
        P("seq", "hid"),
        P("seq", "hid"),
        P(None, "hid"),
        P("hid", "seq"),
        P(),
        P(),
        P(),
        P(),
    )
    return jax.shard_map(
        functools.partial(on_device, mesh.shape["seq"] // 2),
        mesh=mesh, in_specs=placed, out_specs=P("seq", "hid"), check_vma=False,
    )
```

```python
import functools
import math

import jax
import jax.numpy as jnp
from jax import lax
from jax.experimental import pallas as pl
from jax.experimental.pallas import tpu as pltpu
from jax.sharding import PartitionSpec as P

HEAD_DIM = 128
TILE = 384
SLOTS = 6
GROUP = 256
W_CHUNK = 512
UNIT = 384
RING_START = 4
RING_GROUPS = (6,)
RING_CHUNKS = (0, 2, 5)
EXP_SCALE = math.log2(math.e) / math.sqrt(HEAD_DIM)
MESH = pl.DeviceIdType.MESH


def block_kernel(
    chips,
    q_ref, res_ref, scale_ref, gate_ref, slot_ref, list_ref, k_hbm, v_hbm, win_hbm, wout_hbm,
    out_ref,
    kv, wout, win, comb, normed, hidden, term_out, term_in, term_home,
    local_sem, win_sem, near_s, near_r, far_s, far_r, own_s, own_r, cn_s, cn_r, cf_s, cf_r,
    x_s, x_r, ring_s, ring_r, cring_s, cring_r, wown_s, wown_r, term_s, term_r,
):
    seq = lax.axis_index("seq")
    hid = lax.axis_index("hid")
    chip, core = seq // 2, seq % 2
    odd = chip % 2
    rows, width = q_ref.shape
    depth = win_hbm.shape[0]
    units = win_hbm.shape[1]
    groups = width // GROUP
    w_rows = wout_hbm.shape[0]
    half_ring = chips // 2
    last = 2 * (half_ring - 1)
    by_arrival = 2 * w_rows == UNIT

    def at(chip_index, core_index):
        return {"seq": chip_index * 2 + core_index}

    mate = at(chip, 1 - core)
    near = at(chip + 1 - 2 * odd, core)
    step = 2 - 4 * odd
    has_far = (chip - step >= 0) & (chip - step < chips)
    has_fwd = (chip + step >= 0) & (chip + step < chips)
    ahead = at(chip + step, core)
    behind = at(chip - step, core)
    peer = {"hid": 1 - hid}

    place = jnp.where(odd == 0, chip // 2, chips - 1 - chip // 2)

    def ring_chip(position):
        position = (position + 2 * chips) % chips
        return jnp.where(position < half_ring, 2 * position, 2 * (chips - 1 - position) + 1)

    ring_next = at(ring_chip(place + 1), core)
    ring_prev = at(ring_chip(place - 1), core)

    near_row = (4 - 4 * odd) * TILE
    far_row = 4 * odd * TILE
    mid_row = 2 * TILE

    def kv_rows(base, which):
        return pl.ds(pl.multiple_of(base + which * TILE, TILE), TILE)

    def cols(g):
        return pl.ds(pl.multiple_of(g * GROUP, GROUP), GROUP)

    def remote(src, dst, send, recv, device):
        return pltpu.make_async_remote_copy(
            src_ref=src, dst_ref=dst, send_sem=send, recv_sem=recv,
            device_id=device, device_id_type=MESH,
        )

    def mine(g):
        return kv.at[:, kv_rows(mid_row, core), cols(g)]

    def near_copy(g):
        return remote(
            mine(g), kv.at[:, kv_rows(far_row, core), cols(g)], near_s.at[g], near_r.at[g], near
        )

    def far_copy(g):
        return remote(
            kv.at[:, kv_rows(near_row, core), cols(g)],
            kv.at[:, kv_rows(far_row, core), cols(g)], far_s.at[g], far_r.at[g], ahead,
        )

    def mate_copy(base, send, recv, g):
        part = kv.at[:, kv_rows(base, core), cols(g)]
        return remote(part, part, send.at[g], recv.at[g], mate)

    def own_copy(g):
        return mate_copy(mid_row, own_s, own_r, g)

    def cn_copy(g):
        return mate_copy(near_row, cn_s, cn_r, g)

    def cf_copy(g):
        return mate_copy(far_row, cf_s, cf_r, g)

    def comb_cols(g):
        return pl.ds(pl.multiple_of(hid * width + g * GROUP, GROUP), GROUP)

    def x_copy(g):
        part = comb.at[:, comb_cols(g)]
        return remote(part, part, x_s.at[g], x_r.at[g], peer)

    def wout_part(chip_index, core_index, lanes):
        row = pl.multiple_of((chip_index * 2 + core_index) * w_rows, w_rows)
        return wout.at[pl.ds(row, w_rows), lanes]

    def ring_part(way, s, away, core_index):
        half = way if s == last else s % 2
        source = ring_chip(place - away if way == 0 else place + away)
        return wout_part(source, core_index, pl.ds(half * (units // 2), units // 2))

    def ring_copy(way, s):
        part = ring_part(way, s, s // 2, core)
        return remote(
            part, part, ring_s.at[way, s], ring_r.at[way, s],
            ring_next if way == 0 else ring_prev,
        )

    def ring_mate(way, s, core_index):
        part = ring_part(way, s, s // 2 + 1, core_index)
        return remote(part, part, cring_s.at[way, s], cring_r.at[way, s], mate)

    def ring_step(s):
        for way in range(2):
            ring_copy(way, s).wait_recv()
            if s + 2 < last:
                ring_copy(way, s + 2).start()
            elif s < last and s % 2 == way:
                ring_copy(way, last).start()
            ring_mate(way, s, core).start()

    def wown_copy():
        part = wout_part(chip, core, pl.ds(0, units))
        return remote(part, part, wown_s.at[0], wown_r.at[0], mate)

    def win_copy(j, slot):
        return pltpu.make_async_copy(
            win_hbm.at[:, pl.ds(pl.multiple_of(j * W_CHUNK, W_CHUNK), W_CHUNK)],
            win.at[slot], win_sem.at[slot],
        )

    def term_copy(j):
        return remote(term_out.at[j], term_in.at[j], term_s.at[j], term_r.at[j], peer)

    loads = [
        pltpu.make_async_copy(k_hbm, kv.at[0, kv_rows(mid_row, core), :], local_sem.at[0]),
        pltpu.make_async_copy(v_hbm, kv.at[1, kv_rows(mid_row, core), :], local_sem.at[1]),
        pltpu.make_async_copy(
            wout_hbm, wout_part(chip, core, pl.ds(0, units)), local_sem.at[2]
        ),
    ]
    for load in loads:
        load.start()
    win_copy(0, 0).start()
    win_copy(1, 1).start()

    barrier = pltpu.get_barrier_semaphore()
    for device in (mate, near, peer, ring_next, ring_prev):
        pl.semaphore_signal(barrier, inc=1, device_id=device, device_id_type=MESH)

    @pl.when(has_fwd)
    def _():
        pl.semaphore_signal(barrier, inc=1, device_id=ahead, device_id_type=MESH)

    @pl.when(has_far)
    def _():
        pl.semaphore_signal(barrier, inc=1, device_id=behind, device_id_type=MESH)

    pl.semaphore_wait(barrier, 5 + has_fwd.astype(jnp.int32) + has_far.astype(jnp.int32))

    loads[0].wait()
    loads[1].wait()

    def send_own(g, _):
        near_copy(g).start()
        own_copy(g).start()
        return 0

    lax.fori_loop(0, groups, send_own, 0)
    loads[2].wait()
    wown_copy().start()

    masks = []
    tiles = slot_ref.shape[0]
    own_tile = slot_ref[seq]
    for i in range(SLOTS):
        slot = 2 * chip - 2 + i
        inside = ((slot >= 0) & (slot < tiles)).astype(jnp.int32)
        tile = slot_ref[jnp.clip(slot, 0, tiles - 1)]
        hits = jnp.int32(0)
        for j in range(list_ref.shape[1]):
            hits = hits + (list_ref[own_tile, j] == tile).astype(jnp.int32)
        masks.append(jnp.where(hits * inside > 0, jnp.float32(0.0), jnp.float32(-jnp.inf)))

    @pl.when(jnp.logical_not(has_far))
    def _():
        kv[:, pl.ds(pl.multiple_of(far_row, TILE), 2 * TILE), :] = jnp.zeros(
            (2, 2 * TILE, width), kv.dtype
        )

    def attend(g):
        def head(h, _):
            lanes = pl.ds(pl.multiple_of(g * GROUP + h * HEAD_DIM, HEAD_DIM), HEAD_DIM)
            query = q_ref[:, lanes]
            scores = []
            for i in range(0, SLOTS, 2):
                pair = lax.dot_general(
                    query, kv[0, i * TILE : (i + 2) * TILE, lanes], (((1,), (1,)), ((), ())),
                    preferred_element_type=jnp.float32,
                )
                scores += [pair[:, :TILE], pair[:, TILE:]]
            row_max = functools.reduce(
                jnp.maximum,
                [jnp.max(s, axis=-1, keepdims=True) + b for s, b in zip(scores, masks)],
            )
            total = mixed = 0.0
            for i in range(0, SLOTS, 2):
                halves = []
                for k in (i, i + 1):
                    probs = jnp.exp2((scores[k] - (row_max - masks[k])) * EXP_SCALE)
                    total = total + jnp.sum(probs, axis=-1, keepdims=True)
                    halves.append(probs.astype(jnp.bfloat16))
                mixed = mixed + jnp.dot(
                    jnp.concatenate(halves, axis=1), kv[1, i * TILE : (i + 2) * TILE, lanes],
                    preferred_element_type=jnp.float32,
                )
            attn = (mixed / total).astype(jnp.bfloat16)
            summed = res_ref[:, lanes].astype(jnp.float32) + attn.astype(jnp.float32)
            lanes_to = pl.ds(
                pl.multiple_of(hid * width + g * GROUP + h * HEAD_DIM, HEAD_DIM), HEAD_DIM
            )
            comb[:, lanes_to] = summed.astype(jnp.bfloat16)
            return 0

        lax.fori_loop(0, GROUP // HEAD_DIM, head, 0)

    def group_step(g, _):
        @pl.when(g < groups)
        def _():
            near_in = remote(
                mine(g), kv.at[:, kv_rows(near_row, core), cols(g)], near_s.at[g], near_r.at[g],
                near,
            )
            near_in.wait_recv()

            @pl.when(has_fwd)
            def _():
                far_copy(g).start()

            cn_copy(g).start()

        @pl.when(g == RING_START)
        def _():
            for s in range(2):
                ring_copy(0, s).start()
                ring_copy(1, s).start()

        @pl.when(g >= 1)
        def _():
            prior = g - 1

            @pl.when(has_far)
            def _():
                far_copy(prior).wait_recv()
                cf_copy(prior).start()

            mate_in(own_r, mid_row, prior).wait_recv()
            mate_in(cn_r, near_row, prior).wait_recv()

            @pl.when(has_far)
            def _():
                mate_in(cf_r, far_row, prior).wait_recv()

            attend(prior)
            x_copy(prior).start()

        for s, when in enumerate(RING_GROUPS):
            @pl.when(g == when)
            def _(s=s):
                ring_step(s)

        return 0

    def mate_in(recv, base, g):
        part = kv.at[:, kv_rows(base, 1 - core), cols(g)]
        return remote(part, part, own_s.at[g], recv.at[g], mate)

    lax.fori_loop(0, groups + 1, group_step, 0)

    def x_in(g, _):
        part = comb.at[:, pl.ds(pl.multiple_of((1 - hid) * width + g * GROUP, GROUP), GROUP)]
        remote(part, part, x_s.at[g], x_r.at[g], peer).wait_recv()
        return 0

    lax.fori_loop(0, groups, x_in, 0)

    norm_rows = 64

    def norm(i, _):
        block = pl.ds(pl.multiple_of(i * norm_rows, norm_rows), norm_rows)
        wide = comb[block, :].astype(jnp.float32)
        square = jnp.mean(wide * wide, axis=-1, keepdims=True)
        normed[block, :] = (
            wide * lax.rsqrt(square + 1e-06) * (1.0 + scale_ref[...])
        ).astype(jnp.bfloat16)
        return 0

    lax.fori_loop(0, rows // norm_rows, norm, 0)

    w_chunks = units // W_CHUNK

    def project(j, _):
        slot = j % 2
        win_copy(j, slot).wait()
        inner = jnp.dot(normed[...], win[slot], preferred_element_type=jnp.float32)
        hidden[:, pl.ds(pl.multiple_of(j * W_CHUNK, W_CHUNK), W_CHUNK)] = jax.nn.gelu(
            inner, approximate=True
        ).astype(jnp.bfloat16)

        @pl.when(j + 2 < w_chunks)
        def _():
            win_copy(j + 2, slot).start()

        for s, when in enumerate(RING_CHUNKS):
            @pl.when(j == when)
            def _():
                ring_step(len(RING_GROUPS) + s)

        return 0

    lax.fori_loop(0, w_chunks, project, 0)

    handled = len(RING_GROUPS) + len(RING_CHUNKS)
    wown_in = wout_part(chip, 1 - core, pl.ds(0, units))

    def arrived(t):
        if t == 0:
            remote(wown_in, wown_in, wown_s.at[0], wown_r.at[0], mate).wait_recv()
            return
        for s in range(2 * t - 2, min(2 * t, last + 1)):
            for way in range(2):
                ring_mate(way, s, 1 - core).wait_recv()

    out_units = width // UNIT

    def terms(first, j):
        row = pl.multiple_of(first + j * UNIT, UNIT)
        return lax.dot_general(
            hidden[...], wout[pl.ds(row, UNIT), :], (((1,), (1,)), ((), ())),
            preferred_element_type=jnp.float32,
        )

    def send_terms(j):
        term_out[j] = terms((1 - hid) * width, j).astype(jnp.bfloat16)
        term_copy(j).start()

    def finish(j):
        term_copy(j).wait_recv()
        lanes = pl.ds(pl.multiple_of(hid * width + j * UNIT, UNIT), UNIT)
        mlp = term_home[j] + term_in[j].astype(jnp.float32)
        out_ref[:, pl.ds(pl.multiple_of(j * UNIT, UNIT), UNIT)] = (
            comb[:, lanes].astype(jnp.float32) + gate_ref[:, lanes] * mlp
        ).astype(jnp.bfloat16)

    def blocks_at(t):
        if t == 0:
            return [chip]
        if t == half_ring:
            return [ring_chip(place + t)]
        return [ring_chip(place - t), ring_chip(place + t)]

    if by_arrival:
        for t in range(half_ring + 1):
            if t > 0:
                while handled < min(2 * t, last + 1):
                    ring_step(handled)
                    handled += 1
            arrived(t)
            for block in blocks_at(t):
                home = block // out_units == hid
                j = block % out_units

                @pl.when(jnp.logical_not(home))
                def _():
                    send_terms(j)

                @pl.when(home)
                def _():
                    term_home[j] = terms(hid * width, j)

            for block in blocks_at(t - 1) if t > 0 else []:
                @pl.when(block // out_units == hid)
                def _():
                    finish(block % out_units)

        for block in blocks_at(half_ring):
            @pl.when(block // out_units == hid)
            def _():
                finish(block % out_units)
    else:
        for s in range(handled, last + 1):
            ring_step(s)
        for t in range(half_ring + 1):
            arrived(t)

        def away(j, _):
            send_terms(j)
            return 0

        lax.fori_loop(0, out_units, away, 0)

        def at_home(j, _):
            term_home[j] = terms(hid * width, j)
            finish(j)
            return 0

        lax.fori_loop(0, out_units, at_home, 0)

    def sent(g, _):
        near_copy(g).wait_send()
        own_copy(g).wait_send()
        cn_copy(g).wait_send()
        x_copy(g).wait_send()

        @pl.when(has_fwd)
        def _():
            far_copy(g).wait_send()

        @pl.when(has_far)
        def _():
            cf_copy(g).wait_send()

        return 0

    lax.fori_loop(0, groups, sent, 0)
    for s in range(last + 1):
        for way in range(2):
            ring_copy(way, s).wait_send()
            ring_mate(way, s, core).wait_send()
    wown_copy().wait_send()

    def term_sent(j, _):
        term_copy(j).wait_send()
        return 0

    lax.fori_loop(0, out_units, term_sent, 0)


def on_device(
    chips, queries, keys, values, residual, w_in, w_out, mod_scale, mod_gate, slot_tiles, key_tiles
):
    rows, width = queries.shape
    depth, units = w_in.shape
    groups = width // GROUP
    out_units = width // UNIT
    vmem = pl.BlockSpec(memory_space=pltpu.VMEM)
    smem = pl.BlockSpec(memory_space=pltpu.SMEM)
    hbm = pl.BlockSpec(memory_space=pl.ANY)
    dma = pltpu.SemaphoreType.DMA
    half_ring = chips // 2
    return pl.pallas_call(
        functools.partial(block_kernel, chips),
        out_shape=jax.ShapeDtypeStruct((rows, width), jnp.bfloat16),
        in_specs=[vmem] * 4 + [smem] * 2 + [hbm] * 4,
        out_specs=vmem,
        scratch_shapes=[
            pltpu.VMEM((2, SLOTS * TILE, width), jnp.bfloat16),
            pltpu.VMEM((depth, units), jnp.bfloat16),
            pltpu.VMEM((2, depth, W_CHUNK), jnp.bfloat16),
            pltpu.VMEM((rows, depth), jnp.bfloat16),
            pltpu.VMEM((rows, depth), jnp.bfloat16),
            pltpu.VMEM((rows, units), jnp.bfloat16),
            pltpu.VMEM((out_units, rows, UNIT), jnp.bfloat16),
            pltpu.VMEM((out_units, rows, UNIT), jnp.bfloat16),
            pltpu.VMEM((out_units, rows, UNIT), jnp.float32),
            dma((3,)), dma((2,)),
        ] + [dma((groups,))] * 12 + [dma((2, 2 * half_ring - 1))] * 4 + [dma((1,))] * 2
        + [dma((out_units,))] * 2,
        compiler_params=pltpu.CompilerParams(
            collective_id=0, has_side_effects=True, vmem_limit_bytes=62 * 1024 * 1024
        ),
    )(
        queries, residual, mod_scale[None, :], mod_gate[None, :], slot_tiles, key_tiles,
        keys, values, w_in, w_out.T,
    )


def solution(mesh):
    placed = (
        P("seq", "hid"),
        P("seq", "hid"),
        P("seq", "hid"),
        P("seq", "hid"),
        P(None, "hid"),
        P("hid", "seq"),
        P(),
        P(),
        P(),
        P(),
    )
    return jax.shard_map(
        functools.partial(on_device, mesh.shape["seq"] // 2),
        mesh=mesh, in_specs=placed, out_specs=P("seq", "hid"), check_vma=False,
    )
```

```python
import functools
import math

import jax
import jax.numpy as jnp
from jax import lax
from jax.experimental import pallas as pl
from jax.experimental.pallas import tpu as pltpu
from jax.sharding import PartitionSpec as P

HEAD_DIM = 128
TILE = 384
SLOTS = 6
GROUP = 256
W_CHUNK = 512
UNIT = 384
RING_START = 2
RING_GROUPS = (5, 6)
RING_CHUNKS = (0, 2, 4, 5)
EXP_SCALE = math.log2(math.e) / math.sqrt(HEAD_DIM)
MESH = pl.DeviceIdType.MESH


def block_kernel(
    chips,
    q_ref, res_ref, scale_ref, gate_ref, slot_ref, list_ref, k_hbm, v_hbm, win_hbm, wout_hbm,
    out_ref,
    kv, wout, win, comb, normed, hidden, term_out, term_in, term_home,
    local_sem, win_sem, near_s, near_r, far_s, far_r, own_s, own_r, cn_s, cn_r, cf_s, cf_r,
    x_s, x_r, ring_s, ring_r, cring_s, cring_r, wown_s, wown_r, term_s, term_r,
):
    seq = lax.axis_index("seq")
    hid = lax.axis_index("hid")
    chip, core = seq // 2, seq % 2
    odd = chip % 2
    rows, width = q_ref.shape
    depth = win_hbm.shape[0]
    units = win_hbm.shape[1]
    groups = width // GROUP
    w_rows = wout_hbm.shape[0]
    half_ring = chips // 2
    last = 2 * (half_ring - 1)
    by_arrival = 2 * w_rows == UNIT

    def at(chip_index, core_index):
        return {"seq": chip_index * 2 + core_index}

    mate = at(chip, 1 - core)
    near = at(chip + 1 - 2 * odd, core)
    step = 2 - 4 * odd
    has_far = (chip - step >= 0) & (chip - step < chips)
    has_fwd = (chip + step >= 0) & (chip + step < chips)
    ahead = at(chip + step, core)
    behind = at(chip - step, core)
    peer = {"hid": 1 - hid}

    place = jnp.where(odd == 0, chip // 2, chips - 1 - chip // 2)

    def ring_chip(position):
        position = (position + 2 * chips) % chips
        return jnp.where(position < half_ring, 2 * position, 2 * (chips - 1 - position) + 1)

    ring_next = at(ring_chip(place + 1), core)
    ring_prev = at(ring_chip(place - 1), core)

    near_row = (4 - 4 * odd) * TILE
    far_row = 4 * odd * TILE
    mid_row = 2 * TILE

    def kv_rows(base, which):
        return pl.ds(pl.multiple_of(base + which * TILE, TILE), TILE)

    def cols(g):
        return pl.ds(pl.multiple_of(g * GROUP, GROUP), GROUP)

    def remote(src, dst, send, recv, device):
        return pltpu.make_async_remote_copy(
            src_ref=src, dst_ref=dst, send_sem=send, recv_sem=recv,
            device_id=device, device_id_type=MESH,
        )

    def mine(g):
        return kv.at[:, kv_rows(mid_row, core), cols(g)]

    def near_copy(g):
        return remote(
            mine(g), kv.at[:, kv_rows(far_row, core), cols(g)], near_s.at[g], near_r.at[g], near
        )

    def far_copy(g):
        return remote(
            kv.at[:, kv_rows(near_row, core), cols(g)],
            kv.at[:, kv_rows(far_row, core), cols(g)], far_s.at[g], far_r.at[g], ahead,
        )

    def mate_copy(base, send, recv, g):
        part = kv.at[:, kv_rows(base, core), cols(g)]
        return remote(part, part, send.at[g], recv.at[g], mate)

    def own_copy(g):
        return mate_copy(mid_row, own_s, own_r, g)

    def cn_copy(g):
        return mate_copy(near_row, cn_s, cn_r, g)

    def cf_copy(g):
        return mate_copy(far_row, cf_s, cf_r, g)

    def comb_cols(g):
        return pl.ds(pl.multiple_of(hid * width + g * GROUP, GROUP), GROUP)

    def x_copy(g):
        part = comb.at[:, comb_cols(g)]
        return remote(part, part, x_s.at[g], x_r.at[g], peer)

    def wout_part(chip_index, core_index, lanes):
        row = pl.multiple_of((chip_index * 2 + core_index) * w_rows, w_rows)
        return wout.at[pl.ds(row, w_rows), lanes]

    def ring_part(way, s, away, core_index):
        half = way if s == last else s % 2
        source = ring_chip(place - away if way == 0 else place + away)
        return wout_part(source, core_index, pl.ds(half * (units // 2), units // 2))

    def ring_copy(way, s):
        part = ring_part(way, s, s // 2, core)
        return remote(
            part, part, ring_s.at[way, s], ring_r.at[way, s],
            ring_next if way == 0 else ring_prev,
        )

    def ring_mate(way, s, core_index):
        part = ring_part(way, s, s // 2 + 1, core_index)
        return remote(part, part, cring_s.at[way, s], cring_r.at[way, s], mate)

    def ring_step(s):
        for way in range(2):
            ring_copy(way, s).wait_recv()
            if s + 2 < last:
                ring_copy(way, s + 2).start()
            elif s < last and s % 2 == way:
                ring_copy(way, last).start()
            ring_mate(way, s, core).start()

    def wown_copy():
        part = wout_part(chip, core, pl.ds(0, units))
        return remote(part, part, wown_s.at[0], wown_r.at[0], mate)

    def win_copy(j, slot):
        return pltpu.make_async_copy(
            win_hbm.at[:, pl.ds(pl.multiple_of(j * W_CHUNK, W_CHUNK), W_CHUNK)],
            win.at[slot], win_sem.at[slot],
        )

    def term_copy(j):
        return remote(term_out.at[j], term_in.at[j], term_s.at[j], term_r.at[j], peer)

    loads = [
        pltpu.make_async_copy(k_hbm, kv.at[0, kv_rows(mid_row, core), :], local_sem.at[0]),
        pltpu.make_async_copy(v_hbm, kv.at[1, kv_rows(mid_row, core), :], local_sem.at[1]),
        pltpu.make_async_copy(
            wout_hbm, wout_part(chip, core, pl.ds(0, units)), local_sem.at[2]
        ),
    ]
    for load in loads:
        load.start()
    win_copy(0, 0).start()
    win_copy(1, 1).start()

    barrier = pltpu.get_barrier_semaphore()
    for device in (mate, near, peer, ring_next, ring_prev):
        pl.semaphore_signal(barrier, inc=1, device_id=device, device_id_type=MESH)

    @pl.when(has_fwd)
    def _():
        pl.semaphore_signal(barrier, inc=1, device_id=ahead, device_id_type=MESH)

    @pl.when(has_far)
    def _():
        pl.semaphore_signal(barrier, inc=1, device_id=behind, device_id_type=MESH)

    pl.semaphore_wait(barrier, 5 + has_fwd.astype(jnp.int32) + has_far.astype(jnp.int32))

    loads[0].wait()
    loads[1].wait()

    def send_own(g, _):
        near_copy(g).start()
        own_copy(g).start()
        return 0

    lax.fori_loop(0, groups, send_own, 0)
    loads[2].wait()
    wown_copy().start()

    masks = []
    tiles = slot_ref.shape[0]
    own_tile = slot_ref[seq]
    for i in range(SLOTS):
        slot = 2 * chip - 2 + i
        inside = ((slot >= 0) & (slot < tiles)).astype(jnp.int32)
        tile = slot_ref[jnp.clip(slot, 0, tiles - 1)]
        hits = jnp.int32(0)
        for j in range(list_ref.shape[1]):
            hits = hits + (list_ref[own_tile, j] == tile).astype(jnp.int32)
        masks.append(jnp.where(hits * inside > 0, jnp.float32(0.0), jnp.float32(-jnp.inf)))

    @pl.when(jnp.logical_not(has_far))
    def _():
        kv[:, pl.ds(pl.multiple_of(far_row, TILE), 2 * TILE), :] = jnp.zeros(
            (2, 2 * TILE, width), kv.dtype
        )

    def attend(g):
        def head(h, _):
            lanes = pl.ds(pl.multiple_of(g * GROUP + h * HEAD_DIM, HEAD_DIM), HEAD_DIM)
            query = q_ref[:, lanes]
            scores = []
            for i in range(0, SLOTS, 2):
                pair = lax.dot_general(
                    query, kv[0, i * TILE : (i + 2) * TILE, lanes], (((1,), (1,)), ((), ())),
                    preferred_element_type=jnp.float32,
                )
                scores += [pair[:, :TILE], pair[:, TILE:]]
            row_max = functools.reduce(
                jnp.maximum,
                [jnp.max(s, axis=-1, keepdims=True) + b for s, b in zip(scores, masks)],
            )
            total = mixed = 0.0
            for i in range(0, SLOTS, 2):
                halves = []
                for k in (i, i + 1):
                    probs = jnp.exp2((scores[k] - (row_max - masks[k])) * EXP_SCALE)
                    total = total + jnp.sum(probs, axis=-1, keepdims=True)
                    halves.append(probs.astype(jnp.bfloat16))
                mixed = mixed + jnp.dot(
                    jnp.concatenate(halves, axis=1), kv[1, i * TILE : (i + 2) * TILE, lanes],
                    preferred_element_type=jnp.float32,
                )
            attn = (mixed / total).astype(jnp.bfloat16)
            summed = res_ref[:, lanes].astype(jnp.float32) + attn.astype(jnp.float32)
            lanes_to = pl.ds(
                pl.multiple_of(hid * width + g * GROUP + h * HEAD_DIM, HEAD_DIM), HEAD_DIM
            )
            comb[:, lanes_to] = summed.astype(jnp.bfloat16)
            return 0

        lax.fori_loop(0, GROUP // HEAD_DIM, head, 0)

    def group_step(g, _):
        @pl.when(g < groups)
        def _():
            near_in = remote(
                mine(g), kv.at[:, kv_rows(near_row, core), cols(g)], near_s.at[g], near_r.at[g],
                near,
            )
            near_in.wait_recv()

            @pl.when(has_fwd)
            def _():
                far_copy(g).start()

            cn_copy(g).start()

        @pl.when(g == RING_START)
        def _():
            for s in range(2):
                ring_copy(0, s).start()
                ring_copy(1, s).start()

        @pl.when(g >= 1)
        def _():
            prior = g - 1

            @pl.when(has_far)
            def _():
                far_copy(prior).wait_recv()
                cf_copy(prior).start()

            mate_in(own_r, mid_row, prior).wait_recv()
            mate_in(cn_r, near_row, prior).wait_recv()

            @pl.when(has_far)
            def _():
                mate_in(cf_r, far_row, prior).wait_recv()

            attend(prior)
            x_copy(prior).start()

        for s, when in enumerate(RING_GROUPS):
            @pl.when(g == when)
            def _(s=s):
                ring_step(s)

        return 0

    def mate_in(recv, base, g):
        part = kv.at[:, kv_rows(base, 1 - core), cols(g)]
        return remote(part, part, own_s.at[g], recv.at[g], mate)

    lax.fori_loop(0, groups + 1, group_step, 0)

    def x_in(g, _):
        part = comb.at[:, pl.ds(pl.multiple_of((1 - hid) * width + g * GROUP, GROUP), GROUP)]
        remote(part, part, x_s.at[g], x_r.at[g], peer).wait_recv()
        return 0

    lax.fori_loop(0, groups, x_in, 0)

    norm_rows = 64

    def norm(i, _):
        block = pl.ds(pl.multiple_of(i * norm_rows, norm_rows), norm_rows)
        wide = comb[block, :].astype(jnp.float32)
        square = jnp.mean(wide * wide, axis=-1, keepdims=True)
        normed[block, :] = (
            wide * lax.rsqrt(square + 1e-06) * (1.0 + scale_ref[...])
        ).astype(jnp.bfloat16)
        return 0

    lax.fori_loop(0, rows // norm_rows, norm, 0)

    w_chunks = units // W_CHUNK

    def project(j, _):
        slot = j % 2
        win_copy(j, slot).wait()
        inner = jnp.dot(normed[...], win[slot], preferred_element_type=jnp.float32)
        hidden[:, pl.ds(pl.multiple_of(j * W_CHUNK, W_CHUNK), W_CHUNK)] = jax.nn.gelu(
            inner, approximate=True
        ).astype(jnp.bfloat16)

        @pl.when(j + 2 < w_chunks)
        def _():
            win_copy(j + 2, slot).start()

        for s, when in enumerate(RING_CHUNKS):
            @pl.when(j == when)
            def _():
                ring_step(len(RING_GROUPS) + s)

        return 0

    lax.fori_loop(0, w_chunks, project, 0)

    handled = len(RING_GROUPS) + len(RING_CHUNKS)
    wown_in = wout_part(chip, 1 - core, pl.ds(0, units))

    def arrived(t):
        if t == 0:
            remote(wown_in, wown_in, wown_s.at[0], wown_r.at[0], mate).wait_recv()
            return
        for s in range(2 * t - 2, min(2 * t, last + 1)):
            for way in range(2):
                ring_mate(way, s, 1 - core).wait_recv()

    out_units = width // UNIT

    def terms(first, j):
        row = pl.multiple_of(first + j * UNIT, UNIT)
        return lax.dot_general(
            hidden[...], wout[pl.ds(row, UNIT), :], (((1,), (1,)), ((), ())),
            preferred_element_type=jnp.float32,
        )

    def send_terms(j):
        term_out[j] = terms((1 - hid) * width, j).astype(jnp.bfloat16)
        term_copy(j).start()

    def finish(j):
        term_copy(j).wait_recv()
        lanes = pl.ds(pl.multiple_of(hid * width + j * UNIT, UNIT), UNIT)
        mlp = term_home[j] + term_in[j].astype(jnp.float32)
        out_ref[:, pl.ds(pl.multiple_of(j * UNIT, UNIT), UNIT)] = (
            comb[:, lanes].astype(jnp.float32) + gate_ref[:, lanes] * mlp
        ).astype(jnp.bfloat16)

    def blocks_at(t):
        if t == 0:
            return [chip]
        if t == half_ring:
            return [ring_chip(place + t)]
        return [ring_chip(place - t), ring_chip(place + t)]

    if by_arrival:
        for t in range(half_ring + 1):
            if t > 0:
                while handled < min(2 * t, last + 1):
                    ring_step(handled)
                    handled += 1
            arrived(t)
            for block in blocks_at(t):
                home = block // out_units == hid
                j = block % out_units

                @pl.when(jnp.logical_not(home))
                def _():
                    send_terms(j)

                @pl.when(home)
                def _():
                    term_home[j] = terms(hid * width, j)

            for block in blocks_at(t - 1) if t > 0 else []:
                @pl.when(block // out_units == hid)
                def _():
                    finish(block % out_units)

        for block in blocks_at(half_ring):
            @pl.when(block // out_units == hid)
            def _():
                finish(block % out_units)
    else:
        for s in range(handled, last + 1):
            ring_step(s)
        for t in range(half_ring + 1):
            arrived(t)

        def away(j, _):
            send_terms(j)
            return 0

        lax.fori_loop(0, out_units, away, 0)

        def at_home(j, _):
            term_home[j] = terms(hid * width, j)
            finish(j)
            return 0

        lax.fori_loop(0, out_units, at_home, 0)

    def sent(g, _):
        near_copy(g).wait_send()
        own_copy(g).wait_send()
        cn_copy(g).wait_send()
        x_copy(g).wait_send()

        @pl.when(has_fwd)
        def _():
            far_copy(g).wait_send()

        @pl.when(has_far)
        def _():
            cf_copy(g).wait_send()

        return 0

    lax.fori_loop(0, groups, sent, 0)
    for s in range(last + 1):
        for way in range(2):
            ring_copy(way, s).wait_send()
            ring_mate(way, s, core).wait_send()
    wown_copy().wait_send()

    def term_sent(j, _):
        term_copy(j).wait_send()
        return 0

    lax.fori_loop(0, out_units, term_sent, 0)


def on_device(
    chips, queries, keys, values, residual, w_in, w_out, mod_scale, mod_gate, slot_tiles, key_tiles
):
    rows, width = queries.shape
    depth, units = w_in.shape
    groups = width // GROUP
    out_units = width // UNIT
    vmem = pl.BlockSpec(memory_space=pltpu.VMEM)
    smem = pl.BlockSpec(memory_space=pltpu.SMEM)
    hbm = pl.BlockSpec(memory_space=pl.ANY)
    dma = pltpu.SemaphoreType.DMA
    half_ring = chips // 2
    return pl.pallas_call(
        functools.partial(block_kernel, chips),
        out_shape=jax.ShapeDtypeStruct((rows, width), jnp.bfloat16),
        in_specs=[vmem] * 4 + [smem] * 2 + [hbm] * 4,
        out_specs=vmem,
        scratch_shapes=[
            pltpu.VMEM((2, SLOTS * TILE, width), jnp.bfloat16),
            pltpu.VMEM((depth, units), jnp.bfloat16),
            pltpu.VMEM((2, depth, W_CHUNK), jnp.bfloat16),
            pltpu.VMEM((rows, depth), jnp.bfloat16),
            pltpu.VMEM((rows, depth), jnp.bfloat16),
            pltpu.VMEM((rows, units), jnp.bfloat16),
            pltpu.VMEM((out_units, rows, UNIT), jnp.bfloat16),
            pltpu.VMEM((out_units, rows, UNIT), jnp.bfloat16),
            pltpu.VMEM((out_units, rows, UNIT), jnp.float32),
            dma((3,)), dma((2,)),
        ] + [dma((groups,))] * 12 + [dma((2, 2 * half_ring - 1))] * 4 + [dma((1,))] * 2
        + [dma((out_units,))] * 2,
        compiler_params=pltpu.CompilerParams(
            collective_id=0, has_side_effects=True, vmem_limit_bytes=62 * 1024 * 1024
        ),
    )(
        queries, residual, mod_scale[None, :], mod_gate[None, :], slot_tiles, key_tiles,
        keys, values, w_in, w_out.T,
    )


def solution(mesh):
    placed = (
        P("seq", "hid"),
        P("seq", "hid"),
        P("seq", "hid"),
        P("seq", "hid"),
        P(None, "hid"),
        P("hid", "seq"),
        P(),
        P(),
        P(),
        P(),
    )
    return jax.shard_map(
        functools.partial(on_device, mesh.shape["seq"] // 2),
        mesh=mesh, in_specs=placed, out_specs=P("seq", "hid"), check_vma=False,
    )
```
